32 devices in a mesh: ctx: 4 (over y, x), ep: 8 (over z, core).
Axes of the slice: x: 2, y: 2, z: 4, core: 2. Of those that a mesh axis runs over, the one named last changes fastest.
Arguments:
- queries: bfloat16 [8, 512, 4096], P('ep', 'ctx'), may hold values from -150 to 150
- key_heads: bfloat16 [8, 512, 256], P('ep', 'ctx'), may hold values from -6 to 6
- value_head_array: bfloat16 [8, 512, 256], P('ep', 'ctx'), may hold values from -18 to 18
- trace_lengths: int32 [8, 6], P('ep'), may hold values from 1 to 128, 512 in all within a row
- expert_ids: int32 [8, 512, 8], P('ep', 'ctx'), may hold values from 0 to 127, all different within a row; in each aligned block of 128 rows (0 to 127, 128 to 255, ..., all dimensions but the last counted through in order) at most 10 rows name the same one
- gate_weights: float32 [8, 512, 8], P('ep', 'ctx'), may hold values from 0.1 to 1
- norm_gain: bfloat16 [4096], replicated, may hold values from 0.099609375 to 1.8984375
- w_gate: bfloat16 [4096, 12288], P('ctx', 'ep'), may hold values from -0.09375 to 0.09375
- w_up: bfloat16 [4096, 12288], P('ctx', 'ep'), may hold values from -0.09375 to 0.09375
- w_down: bfloat16 [12288, 4096], P('ep', 'ctx'), may hold values from -0.15625 to 0.15625
Outputs:
- layer_out: bfloat16 [8, 512, 4096], P('ep', 'ctx')
The draws below stay inside these ranges and needn't reach their ends.
Inputs may be any that keep to these rules, and one draw needn't show every extreme that they name: `expert_ids`: the 8 ids of a row differ; among the 128 rows of one device no id is named more than 10 times.
All inputs are finite; a program needn't handle non-finite values.
Results may differ from the reference program's by a relative error of at most 0.0042.
Values may be sent and summed in bfloat16 or wider, within the bound.
A program may use at most 128 MiB of HBM per device.

```python
import math
import jax
import jax.numpy as jnp
import numpy as np
from jax import lax

D = 4096
HEAD_SIZE = 128
QUERY_HEADS = 32
KEY_VALUE_HEADS = 2
EXPERTS = 128
TOPK = 8
EXP_WIN = 8
FF_WIN = 1536
TOK_DEV = 128
TRACES = 6
ROW_LENGTH = 512
PACKED_BATCH = 8
TRACE_MAX = 128
CAP = 10
FF_DEV = 1536
N_CTX = 4
N_EP = 8


def paired_rows(key):
    first_index = jax.random.fold_in(key, 0)
    drawn_result = jax.random.normal(first_index, (PACKED_BATCH, ROW_LENGTH, KEY_VALUE_HEADS * HEAD_SIZE), jnp.float32)
    return jnp.clip(drawn_result, -6.0, 6.0)


def draw_key_heads(key, part):
    return paired_rows(key).astype(jnp.bfloat16)


def draw_queries(key, part):
    key = jax.random.fold_in(key, 7)
    first_index = jax.random.fold_in(key, 0)
    random_jitter = jax.random.normal(first_index, (PACKED_BATCH, ROW_LENGTH, QUERY_HEADS * HEAD_SIZE), jnp.float32)
    return jnp.clip(random_jitter, -6.0, 6.0).astype(jnp.bfloat16)


def shard_levels(rng, dims, cuts, least, high):
    def one(position, blocks):
        heights = jax.random.uniform(jax.random.fold_in(jax.random.fold_in(rng, 6), position), (blocks,), jnp.float32, least / len(cuts), high / len(cuts))
        return jnp.repeat(jnp.exp(heights), dims[position] // blocks).reshape((-1,) + (1,) * (len(dims) - position - 1))

    level = one(*cuts[0])
    for cut in cuts[1:]:
        level = level * one(*cut)
    return level


def split_up(count, total, reach, skew):
    loads = [(1 << 20) // math.isqrt(standing ** skew) + 1 for standing in range(2, count + 1)]
    rest, given = total - reach - (count - 1), [1] * (count - 1)
    while rest > 0:
        candidates = [i for i in range(count - 1) if given[i] < reach]
        pool, remaining = sum([loads[i] for i in candidates]), rest
        for i in candidates:
            more = min(reach - given[i], max(1, remaining * loads[i] // pool), rest)
            given[i] = given[i] + more
            rest = rest - more
    return np.array([reach] + given)


def ragged_sizes(stream_key, number_of, total, bound, lean):
    if number_of == 2:
        one = jax.random.randint(stream_key, (), max(1, total - bound), min(bound, total - 1) + 1)
        return jnp.stack([one, total - one])
    sizes = jnp.asarray(split_up(number_of, total, bound, lean), jnp.int32)
    pairs = (number_of - 1) // 2
    donor, sink = sizes[1:1 + 2 * pairs:2], sizes[2:2 + 2 * pairs:2]
    margin = jnp.minimum(donor - 1, bound - sink)
    moved = jax.random.randint(jax.random.fold_in(stream_key, 1), (pairs,), 0, 1 << 20) % (margin + 1)
    sizes = sizes.at[1:1 + 2 * pairs:2].set(donor - moved).at[2:2 + 2 * pairs:2].set(sink + moved)
    return sizes[jax.random.permutation(jax.random.fold_in(stream_key, 2), number_of)]


def shared_out(stream_key, own, number, rows, number_of, top, reach, slope):
    sequence = jax.random.permutation(stream_key, number_of)
    packed, usual = shares(number_of, rows * top, reach, slope, True), shares(number_of, rows * top, reach, slope, False)
    places = jnp.arange(number_of)

    def named(lengths, turn):
        used = int((lengths > 0).sum())
        fixed = max(1, used // 4)
        moved = fixed + (places - fixed + turn * (used - fixed)) % max(1, number_of - fixed)
        return jnp.zeros((number_of,), jnp.int32).at[sequence[jnp.where(places < fixed, places, moved)]].set(jnp.asarray(lengths, jnp.int32))

    lengths = jnp.where(number % 4 == 0, named(packed, number // 4), named(usual, number - number // 4 - 1))
    mixed = jax.random.permutation(jax.random.fold_in(own, 3), number_of)
    source_of, sink = mixed[0:number_of // 2 * 2:2], mixed[1:number_of // 2 * 2:2]
    room = jnp.minimum(lengths[source_of] - 1, reach - lengths[sink]) // 2
    room = jnp.where((source_of == sequence[0]) | (sink == sequence[0]) | (lengths[sink] == 0), 0, jnp.maximum(room, 0))
    moved = jax.random.randint(jax.random.fold_in(own, 4), (number_of // 2,), 0, 1 << 20) % (room + 1)
    lengths = lengths.at[source_of].add(-moved).at[sink].add(moved)
    labels = jnp.searchsorted(jnp.cumsum(lengths), jnp.arange(rows * top), side="right").astype(jnp.int32)
    table = labels.reshape(top, rows).T
    table = table[jax.random.permutation(jax.random.fold_in(own, 1), rows)]
    turn = jax.random.randint(jax.random.fold_in(own, 2), (rows, 1), 0, top)
    return jnp.take_along_axis(table, (jnp.arange(top)[None, :] + turn) % top, axis=1)


def shares(number_of, total, most, slope, full):
    loads = [(1 << 20) // math.isqrt(grade ** slope) + 1 for grade in range(1, number_of + 1)]
    largest = most if full else min(most, max(-(-total // number_of), total * loads[0] // sum(loads)))
    least = 1 if total - largest >= number_of - 1 else 0
    given, surplus = [largest] + [least] * (number_of - 1), total - largest - least * (number_of - 1)
    while surplus > 0:
        free = [i for i in range(1, number_of) if given[i] < largest] or [i for i in range(1, number_of) if given[i] < most]
        pool, left = sum([loads[i] for i in free]), surplus
        for i in free:
            addition = min(most - given[i], max(1, left * loads[i] // pool), surplus)
            given[i] = given[i] + addition
            surplus = surplus - addition
    return np.array(given)


def gaussian(stream_key, extent, scale, most, shards=(), kind=jnp.bfloat16):
    factor_of = shard_levels(stream_key, extent, shards, -0.22, 0.18) if shards else 1.0
    drawn = jax.random.normal(stream_key, extent, jnp.float32) * scale * factor_of
    return jnp.minimum(jnp.maximum(drawn, -most), most).astype(kind)


def setup_inputs(seed: int = 0) -> dict:
    key_of = jax.random.split(jax.random.key(seed), 11)
    queries = draw_queries(jax.random.fold_in(key_of[10], 71), 0)
    key_heads = draw_key_heads(jax.random.fold_in(key_of[10], 71), 0)
    value_head_array = gaussian(key_of[2], (PACKED_BATCH, ROW_LENGTH, KEY_VALUE_HEADS * HEAD_SIZE), 3.0, 18.0, ((0, 8), (1, 4)))
    trace_lengths = jax.vmap(lambda own: ragged_sizes(own, TRACES, ROW_LENGTH, TRACE_MAX, 2))(jax.random.split(key_of[3], PACKED_BATCH)).reshape((PACKED_BATCH, TRACES)).astype(jnp.int32)
    expert_ids_keys = jax.random.split(jax.random.fold_in(key_of[4], 1), PACKED_BATCH * ROW_LENGTH // TOK_DEV)
    expert_ids_turns = jax.random.permutation(jax.random.fold_in(key_of[4], 3), PACKED_BATCH * ROW_LENGTH // TOK_DEV)
    expert_ids = jax.vmap(lambda own, number: shared_out(jax.random.fold_in(key_of[4], 2), own, number, TOK_DEV, EXPERTS, TOPK, CAP, 2))(expert_ids_keys, expert_ids_turns).reshape((PACKED_BATCH, ROW_LENGTH, TOPK))
    gate_weights = jnp.clip(0.1 + 0.9 * jax.random.uniform(key_of[5], (PACKED_BATCH, ROW_LENGTH, TOPK), jnp.float32) ** shard_levels(key_of[5], (PACKED_BATCH, ROW_LENGTH, TOPK), ((0, 8), (1, 4)), -0.2, 0.2), 0.1, 1.0)
    norm_gain = jnp.clip(1.0 + 0.18 * jax.random.normal(key_of[6], (D,), jnp.float32), 0.099609375, 1.8984375).astype(jnp.bfloat16)
    w_gate = gaussian(key_of[7], (D, EXP_WIN * FF_WIN), D ** -0.5, 0.09375, ((0, 4), (1, 8)))
    w_up = gaussian(key_of[8], (D, EXP_WIN * FF_WIN), D ** -0.5, 0.09375, ((0, 4), (1, 8)))
    w_down = gaussian(key_of[9], (EXP_WIN * FF_WIN, D), FF_WIN ** -0.5, 0.15625, ((0, 8), (1, 4)))
    return dict(queries=queries, key_heads=key_heads, value_head_array=value_head_array, trace_lengths=trace_lengths, expert_ids=expert_ids, gate_weights=gate_weights, norm_gain=norm_gain, w_gate=w_gate, w_up=w_up, w_down=w_down)


def trace_first(trace_lengths, positions):
    trace_ends = jnp.cumsum(trace_lengths, axis=-1)
    starts = trace_ends - trace_lengths
    return lax.optimization_barrier(jnp.max(jnp.where(starts[..., None, :] <= positions[:, None], starts[..., None, :], 0), axis=-1))

def reference(queries, key_heads, value_head_array, trace_lengths, expert_ids, gate_weights, norm_gain, w_gate, w_up, w_down):
    head_groups = QUERY_HEADS // KEY_VALUE_HEADS
    block_index = min(512, ROW_LENGTH)
    score_scale = 1.0 / math.sqrt(HEAD_SIZE)
    positions = jnp.arange(ROW_LENGTH, dtype=jnp.int32)
    first_pos = trace_first(trace_lengths, positions).astype(jnp.int32)

    def one_row(operands):
        query_row_slice, key_row_slice, value_row_slice, start_row = operands
        key_division = key_row_slice.astype(jnp.float32).reshape(ROW_LENGTH, KEY_VALUE_HEADS, HEAD_SIZE)
        value_division = value_row_slice.astype(jnp.float32).reshape(ROW_LENGTH, KEY_VALUE_HEADS, HEAD_SIZE)
        query_block_list = query_row_slice.reshape(ROW_LENGTH // block_index, block_index, KEY_VALUE_HEADS, head_groups, HEAD_SIZE)

        def one_block(index):
            query_division = lax.dynamic_index_in_dim(query_block_list, index, 0, keepdims=False).astype(jnp.float32)
            scores = jnp.einsum('tkgd,skd->kgts', query_division, key_division) * score_scale
            query_pos = (index * block_index + jnp.arange(block_index, dtype=jnp.int32)).astype(jnp.int32)
            own_first = lax.dynamic_slice_in_dim(start_row, (index * block_index).astype(jnp.int32), block_index)
            visible = (positions[None, :] <= query_pos[:, None]) & (positions[None, :] >= own_first[:, None])
            scores = jnp.where(visible, scores, -1e+30)
            top_score = lax.optimization_barrier(jnp.max(scores, axis=-1, keepdims=True))
            weights = jnp.where(visible, jnp.exp(scores - top_score), 0.0)
            totals = lax.optimization_barrier(jnp.sum(weights, axis=-1))
            rounded = lax.optimization_barrier(weights.astype(jnp.bfloat16)).astype(jnp.float32)
            summed = jnp.einsum('kgts,skd->kgtd', rounded, value_division)
            return (summed / totals[..., None]).transpose(2, 0, 1, 3).reshape(block_index, QUERY_HEADS * HEAD_SIZE)
        return lax.map(one_block, jnp.arange(ROW_LENGTH // block_index, dtype=jnp.int32)).reshape(ROW_LENGTH, QUERY_HEADS * HEAD_SIZE)
    context = lax.map(one_row, (queries, key_heads, value_head_array, first_pos))
    mean_square = lax.optimization_barrier(jnp.mean(context * context, axis=-1, keepdims=True))
    normed = (context * lax.rsqrt(mean_square + 1e-06) * norm_gain.astype(jnp.float32)).astype(jnp.bfloat16)
    blocks = PACKED_BATCH * N_CTX
    normed_blocks = normed.reshape(blocks, TOK_DEV, D)
    chosen_ids = expert_ids.reshape(blocks, TOK_DEV, TOPK)
    weight_rows = gate_weights.reshape(blocks, TOK_DEV, TOPK).astype(jnp.float32)
    slab_size = N_EP // EXP_WIN
    slot_range = jnp.arange(CAP, dtype=jnp.int32)
    token_range = jnp.arange(TOK_DEV, dtype=jnp.int32)
    expert_mix = jnp.zeros((blocks, TOK_DEV, D), jnp.float32)
    for e in range(EXP_WIN):
        chosen = chosen_ids == e
        routed = jnp.any(chosen, axis=-1)
        gate = lax.optimization_barrier(jnp.sum(jnp.where(chosen, weight_rows, 0.0), axis=-1))
        slot_index = (jnp.cumsum(routed.astype(jnp.int32), axis=1, dtype=jnp.int32) - 1).astype(jnp.int32)
        taken = (slot_index[:, None, :] == slot_range[None, :, None]) & routed[:, None, :]
        source = lax.optimization_barrier(jnp.sum(jnp.where(taken, token_range[None, None, :], 0), axis=-1)).astype(jnp.int32)
        filled = jnp.any(taken, axis=-1)
        picked_rows = jnp.take_along_axis(normed_blocks, source[..., None], axis=1)
        picked_rows = jnp.where(filled[..., None], picked_rows, jnp.zeros((), jnp.bfloat16))
        flat_rows = picked_rows.reshape(blocks * CAP, D)
        gate_proj = jnp.dot(flat_rows, w_gate[:, e * FF_WIN:(e + 1) * FF_WIN], preferred_element_type=jnp.float32)
        up_proj = jnp.dot(flat_rows, w_up[:, e * FF_WIN:(e + 1) * FF_WIN], preferred_element_type=jnp.float32)
        hidden = (jax.nn.silu(gate_proj) * up_proj).astype(jnp.bfloat16)

        def add_slice(j, running):
            hidden_part = lax.dynamic_slice_in_dim(hidden, (j * FF_DEV).astype(jnp.int32), FF_DEV, 1)
            down_part = lax.dynamic_slice_in_dim(w_down, (e * FF_WIN + j * FF_DEV).astype(jnp.int32), FF_DEV, 0)
            partial_value = jnp.dot(hidden_part, down_part, preferred_element_type=jnp.float32)
            return running + lax.optimization_barrier(partial_value.astype(jnp.bfloat16)).astype(jnp.float32)
        expert_out = lax.fori_loop(0, slab_size, add_slice, jnp.zeros((blocks * CAP, D), jnp.float32))
        out_blocks = expert_out.reshape(blocks, CAP, D)
        picked = jnp.take_along_axis(out_blocks, jnp.maximum(slot_index, 0)[..., None], axis=1)
        expert_mix = expert_mix + gate[..., None] * picked
    return (context + expert_mix.reshape(PACKED_BATCH, ROW_LENGTH, D)).astype(jnp.bfloat16)
```

```python
import math

import jax
import jax.numpy as jnp
from jax import lax
from jax.sharding import PartitionSpec as P

D = 4096
HEAD_SIZE = 128
QUERY_HEADS = 32
KEY_VALUE_HEADS = 2
EXP_WIN = 8
CAP = 10


def shifted(block, axis, distance):
    devices = range(lax.axis_size(axis))
    route = [(i - distance, i) for i in devices if i - distance in devices]
    return lax.ppermute(block, axis, route)


def trace_first(trace_lengths, positions):
    trace_ends = jnp.cumsum(trace_lengths)
    starts = trace_ends - trace_lengths
    return jnp.max(jnp.where(starts[None, :] <= positions[:, None], starts[None, :], 0), axis=1)


def experts(stacked, w_gate, w_up, w_down):
    ep_count = lax.axis_size("ep")
    ctx_count = lax.axis_size("ctx")
    slab_size = ep_count // EXP_WIN
    wide = w_gate.shape[0]
    rows = ep_count * CAP
    outgoing = jnp.repeat(stacked, slab_size, axis=0)
    arrived = lax.all_to_all(outgoing, "ep", split_axis=0, concat_axis=0, tiled=True)
    cut = arrived.reshape(rows, ctx_count, wide).transpose(1, 0, 2)
    cut = lax.all_to_all(cut, "ctx", split_axis=0, concat_axis=0, tiled=True)
    flat = cut.reshape(ctx_count * rows, wide)
    gate_part = jnp.dot(flat, w_gate, preferred_element_type=jnp.float32).astype(jnp.bfloat16)
    up_part = jnp.dot(flat, w_up, preferred_element_type=jnp.float32).astype(jnp.bfloat16)
    both = jnp.stack([gate_part, up_part]).reshape(2, ctx_count, rows, -1)
    both = lax.all_to_all(both, "ctx", split_axis=1, concat_axis=1, tiled=True)
    proj = jnp.sum(both.astype(jnp.float32), axis=1)
    hidden = (jax.nn.silu(proj[0]) * proj[1]).astype(jnp.bfloat16)
    hidden = lax.all_gather(hidden, "ctx", axis=0, tiled=True)
    out = jnp.dot(hidden, w_down, preferred_element_type=jnp.float32).astype(jnp.bfloat16)
    out = lax.all_to_all(
        out.reshape(ctx_count, rows, wide), "ctx", split_axis=0, concat_axis=0, tiled=True
    )
    out = out.transpose(1, 0, 2).reshape(ep_count, CAP, ctx_count * wide)
    returned = lax.all_to_all(out, "ep", split_axis=0, concat_axis=0, tiled=True)
    return returned.astype(jnp.float32).reshape(EXP_WIN, slab_size, CAP, D).sum(axis=1)


def local(
    queries,
    key_heads,
    value_head_array,
    trace_lengths,
    expert_ids,
    gate_weights,
    norm_gain,
    w_gate,
    w_up,
    w_down,
):
    rows_per_shard = queries.shape[1]
    head_groups = QUERY_HEADS // KEY_VALUE_HEADS
    ctx_place = lax.axis_index("ctx")
    ctx_count = lax.axis_size("ctx")
    reach_count = ctx_count // 4
    query_pos = ctx_place * rows_per_shard + jnp.arange(rows_per_shard, dtype=jnp.int32)
    first_pos = trace_first(trace_lengths[0], query_pos)
    query_division = queries[0].reshape(rows_per_shard, KEY_VALUE_HEADS, head_groups, HEAD_SIZE)
    score_scale = 1.0 / math.sqrt(HEAD_SIZE)

    def attend(running, kv_piece, offset):
        key_portion, value_portion = kv_piece
        width = key_portion.shape[1]
        size_value = min(512, width)
        old_max, old_total, old_sum = running
        key_division = key_portion[0, 0:size_value].reshape(size_value, KEY_VALUE_HEADS, HEAD_SIZE)
        value_division = value_portion[0, 0:size_value].reshape(
            size_value, KEY_VALUE_HEADS, HEAD_SIZE
        )
        scores = (
            jnp.einsum(
                "tkgd,skd->kgts", query_division, key_division, preferred_element_type=jnp.float32
            )
            * score_scale
        )
        key_pos = offset + 0 + jnp.arange(size_value, dtype=jnp.int32)
        visible = (key_pos[None, :] <= query_pos[:, None]) & (
            key_pos[None, :] >= first_pos[:, None]
        )
        scores = jnp.where(visible, scores, -1e30)
        new_max = jnp.maximum(old_max, jnp.max(scores, axis=-1))
        weights = jnp.where(visible, jnp.exp(scores - new_max[..., None]), 0.0)
        rescale = jnp.exp(old_max - new_max)
        new_total = old_total * rescale + jnp.sum(weights, axis=-1)
        new_sum = old_sum * rescale[..., None] + jnp.einsum(
            "kgts,skd->kgtd",
            weights.astype(jnp.bfloat16),
            value_division,
            preferred_element_type=jnp.float32,
        )
        running = (new_max, new_total, new_sum)
        return running

    empty_state = (
        jnp.full((KEY_VALUE_HEADS, head_groups, rows_per_shard), -1e30, jnp.float32),
        jnp.zeros((KEY_VALUE_HEADS, head_groups, rows_per_shard), jnp.float32),
        jnp.zeros((KEY_VALUE_HEADS, head_groups, rows_per_shard, HEAD_SIZE), jnp.float32),
    )
    own_pair = jnp.stack([key_heads, value_head_array])
    own_state = attend(empty_state, (key_heads, value_head_array), ctx_place * rows_per_shard)

    def earlier_step(i, state):
        moving, running = state
        moving = shifted(moving, "ctx", 1)
        running = attend(running, (moving[0], moving[1]), (ctx_place - i - 1) * rows_per_shard)
        return (moving, running)

    final_state = lax.fori_loop(0, reach_count, earlier_step, (own_pair, own_state))[1]
    context = (
        (final_state[2] / final_state[1][..., None])
        .transpose(2, 0, 1, 3)
        .reshape(rows_per_shard, QUERY_HEADS * HEAD_SIZE)
    )
    mean_square = jnp.mean(context * context, axis=-1, keepdims=True)
    normed = (context * lax.rsqrt(mean_square + 1e-06) * norm_gain.astype(jnp.float32)).astype(
        jnp.bfloat16
    )
    chosen_ids = expert_ids[0]
    weight_rows = gate_weights[0]
    slot_range = jnp.arange(CAP, dtype=jnp.int32)
    placing_list = []
    mixing_list = []
    for e in range(EXP_WIN):
        chosen = chosen_ids == e
        routed = jnp.any(chosen, axis=-1)
        gate_value = jnp.sum(jnp.where(chosen, weight_rows, 0.0), axis=-1)
        slot_index = jnp.cumsum(routed.astype(jnp.int32)) - 1
        taken = (slot_index[None, :] == slot_range[:, None]) & routed[None, :]
        placing_list.append(taken.astype(jnp.bfloat16))
        mixing_list.append(jnp.where(taken.T, gate_value[:, None], 0.0))
    placing = jnp.concatenate(placing_list, axis=0)
    mixing = jnp.concatenate(mixing_list, axis=1)
    stacked = (
        jnp.dot(placing, normed, preferred_element_type=jnp.float32)
        .astype(jnp.bfloat16)
        .reshape(EXP_WIN, CAP, D)
    )
    expert_out = experts(stacked, w_gate, w_up, w_down)
    expert_mix = jnp.dot(
        mixing,
        expert_out.reshape(EXP_WIN * CAP, D),
        precision=lax.Precision.HIGHEST,
        preferred_element_type=jnp.float32,
    )
    return (context + expert_mix).astype(jnp.bfloat16)[None]


def solution(mesh):
    in_specs = (
        P("ep", "ctx", None),
        P("ep", "ctx", None),
        P("ep", "ctx", None),
        P("ep", None),
        P("ep", "ctx", None),
        P("ep", "ctx", None),
        P(),
        P("ctx", "ep"),
        P("ctx", "ep"),
        P("ep", "ctx"),
    )
    out_specs = P("ep", "ctx", None)
    return jax.shard_map(local, mesh=mesh, in_specs=in_specs, out_specs=out_specs, check_vma=False)
```

```python
import functools
import math

import jax
import jax.numpy as jnp
import numpy as np
from jax import lax
from jax.experimental import pallas as pl
from jax.experimental.pallas import tpu as pltpu
from jax.sharding import PartitionSpec as P

D = 4096
HEAD_SIZE = 128
QUERY_HEADS = 32
KEY_VALUE_HEADS = 2
EXP_WIN = 8
CAP = 10


def shifted(block, axis, distance):
    devices = range(lax.axis_size(axis))
    route = [(i - distance, i) for i in devices if i - distance in devices]
    return lax.ppermute(block, axis, route)


def trace_first(trace_lengths, positions):
    trace_ends = jnp.cumsum(trace_lengths)
    starts = trace_ends - trace_lengths
    return jnp.max(jnp.where(starts[None, :] <= positions[:, None], starts[None, :], 0), axis=1)


def experts(stacked, w_gate, w_up, w_down):
    ep_count = lax.axis_size("ep")
    ctx_count = lax.axis_size("ctx")
    slab_size = ep_count // EXP_WIN
    wide = w_gate.shape[0]
    rows = ep_count * CAP
    outgoing = jnp.repeat(stacked, slab_size, axis=0)
    arrived = lax.all_to_all(outgoing, "ep", split_axis=0, concat_axis=0, tiled=True)
    cut = arrived.reshape(rows, ctx_count, wide).transpose(1, 0, 2)
    cut = lax.all_to_all(cut, "ctx", split_axis=0, concat_axis=0, tiled=True)
    flat = cut.reshape(ctx_count * rows, wide)
    gate_part = jnp.dot(flat, w_gate, preferred_element_type=jnp.float32).astype(jnp.bfloat16)
    up_part = jnp.dot(flat, w_up, preferred_element_type=jnp.float32).astype(jnp.bfloat16)
    both = jnp.stack([gate_part, up_part]).reshape(2, ctx_count, rows, -1)
    both = lax.all_to_all(both, "ctx", split_axis=1, concat_axis=1, tiled=True)
    proj = jnp.sum(both.astype(jnp.float32), axis=1)
    hidden = (jax.nn.silu(proj[0]) * proj[1]).astype(jnp.bfloat16)
    hidden = lax.all_gather(hidden, "ctx", axis=0, tiled=True)
    out = jnp.dot(hidden, w_down, preferred_element_type=jnp.float32).astype(jnp.bfloat16)
    out = lax.all_to_all(
        out.reshape(ctx_count, rows, wide), "ctx", split_axis=0, concat_axis=0, tiled=True
    )
    out = out.transpose(1, 0, 2).reshape(ep_count, CAP, ctx_count * wide)
    returned = lax.all_to_all(out, "ep", split_axis=0, concat_axis=0, tiled=True)
    return returned.astype(jnp.float32).reshape(EXP_WIN, slab_size, CAP, D).sum(axis=1)


def local_plain(
    queries,
    key_heads,
    value_head_array,
    trace_lengths,
    expert_ids,
    gate_weights,
    norm_gain,
    w_gate,
    w_up,
    w_down,
):
    rows_per_shard = queries.shape[1]
    head_groups = QUERY_HEADS // KEY_VALUE_HEADS
    ctx_place = lax.axis_index("ctx")
    ctx_count = lax.axis_size("ctx")
    reach_count = ctx_count // 4
    query_pos = ctx_place * rows_per_shard + jnp.arange(rows_per_shard, dtype=jnp.int32)
    first_pos = trace_first(trace_lengths[0], query_pos)
    query_division = queries[0].reshape(rows_per_shard, KEY_VALUE_HEADS, head_groups, HEAD_SIZE)
    score_scale = 1.0 / math.sqrt(HEAD_SIZE)

    def attend(running, kv_piece, offset):
        key_portion, value_portion = kv_piece
        width = key_portion.shape[1]
        size_value = min(512, width)
        old_max, old_total, old_sum = running
        key_division = key_portion[0, 0:size_value].reshape(size_value, KEY_VALUE_HEADS, HEAD_SIZE)
        value_division = value_portion[0, 0:size_value].reshape(
            size_value, KEY_VALUE_HEADS, HEAD_SIZE
        )
        scores = (
            jnp.einsum(
                "tkgd,skd->kgts", query_division, key_division, preferred_element_type=jnp.float32
            )
            * score_scale
        )
        key_pos = offset + 0 + jnp.arange(size_value, dtype=jnp.int32)
        visible = (key_pos[None, :] <= query_pos[:, None]) & (
            key_pos[None, :] >= first_pos[:, None]
        )
        scores = jnp.where(visible, scores, -1e30)
        new_max = jnp.maximum(old_max, jnp.max(scores, axis=-1))
        weights = jnp.where(visible, jnp.exp(scores - new_max[..., None]), 0.0)
        rescale = jnp.exp(old_max - new_max)
        new_total = old_total * rescale + jnp.sum(weights, axis=-1)
        new_sum = old_sum * rescale[..., None] + jnp.einsum(
            "kgts,skd->kgtd",
            weights.astype(jnp.bfloat16),
            value_division,
            preferred_element_type=jnp.float32,
        )
        running = (new_max, new_total, new_sum)
        return running

    empty_state = (
        jnp.full((KEY_VALUE_HEADS, head_groups, rows_per_shard), -1e30, jnp.float32),
        jnp.zeros((KEY_VALUE_HEADS, head_groups, rows_per_shard), jnp.float32),
        jnp.zeros((KEY_VALUE_HEADS, head_groups, rows_per_shard, HEAD_SIZE), jnp.float32),
    )
    own_pair = jnp.stack([key_heads, value_head_array])
    own_state = attend(empty_state, (key_heads, value_head_array), ctx_place * rows_per_shard)

    def earlier_step(i, state):
        moving, running = state
        moving = shifted(moving, "ctx", 1)
        running = attend(running, (moving[0], moving[1]), (ctx_place - i - 1) * rows_per_shard)
        return (moving, running)

    final_state = lax.fori_loop(0, reach_count, earlier_step, (own_pair, own_state))[1]
    context = (
        (final_state[2] / final_state[1][..., None])
        .transpose(2, 0, 1, 3)
        .reshape(rows_per_shard, QUERY_HEADS * HEAD_SIZE)
    )
    mean_square = jnp.mean(context * context, axis=-1, keepdims=True)
    normed = (context * lax.rsqrt(mean_square + 1e-06) * norm_gain.astype(jnp.float32)).astype(
        jnp.bfloat16
    )
    chosen_ids = expert_ids[0]
    weight_rows = gate_weights[0]
    slot_range = jnp.arange(CAP, dtype=jnp.int32)
    placing_list = []
    mixing_list = []
    for e in range(EXP_WIN):
        chosen = chosen_ids == e
        routed = jnp.any(chosen, axis=-1)
        gate_value = jnp.sum(jnp.where(chosen, weight_rows, 0.0), axis=-1)
        slot_index = jnp.cumsum(routed.astype(jnp.int32)) - 1
        taken = (slot_index[None, :] == slot_range[:, None]) & routed[None, :]
        placing_list.append(taken.astype(jnp.bfloat16))
        mixing_list.append(jnp.where(taken.T, gate_value[:, None], 0.0))
    placing = jnp.concatenate(placing_list, axis=0)
    mixing = jnp.concatenate(mixing_list, axis=1)
    stacked = (
        jnp.dot(placing, normed, preferred_element_type=jnp.float32)
        .astype(jnp.bfloat16)
        .reshape(EXP_WIN, CAP, D)
    )
    expert_out = experts(stacked, w_gate, w_up, w_down)
    expert_mix = jnp.dot(
        mixing,
        expert_out.reshape(EXP_WIN * CAP, D),
        precision=lax.Precision.HIGHEST,
        preferred_element_type=jnp.float32,
    )
    return (context + expert_mix).astype(jnp.bfloat16)[None]


LANES = 128
PIECES = 4
MESH = pl.DeviceIdType.MESH


def fused(
    ctx_count,
    ep_count,
    ids_ref,
    ids_t_ref,
    gates_ref,
    lengths_ref,
    q_ref,
    k_ref,
    v_ref,
    gain_ref,
    row_meta_ref,
    col_meta_ref,
    lower_ref,
    upper_ref,
    perm_ref,
    perm_t_ref,
    w_gate_hbm,
    w_up_hbm,
    w_down_hbm,
    out_ref,
    kv_prev,
    context,
    normed,
    tall,
    sent_rows,
    got_rows,
    flat,
    partial,
    got_partial,
    hidden,
    got_hidden,
    turned,
    sent_out,
    got_out,
    expert_out,
    w_gate,
    w_up,
    w_down,
    w_sem,
    kv_send,
    kv_recv,
    rows_send,
    rows_recv,
    part_send,
    part_recv,
    hid_send,
    hid_recv,
    out_send,
    out_recv,
):
    f32, bf16 = jnp.float32, jnp.bfloat16
    c = lax.axis_index("ctx")
    e = lax.axis_index("ep")
    devices = ctx_count * ep_count
    tokens = q_ref.shape[0]
    wide = w_gate.shape[0]
    units = w_gate.shape[1]
    chunks = wide // LANES
    block = chunks * CAP
    slots = ep_count * CAP
    piece = units // PIECES
    head_groups = QUERY_HEADS // KEY_VALUE_HEADS

    weight_copies = [
        pltpu.make_async_copy(hbm, vmem, w_sem.at[i])
        for i, (hbm, vmem) in enumerate(
            ((w_gate_hbm, w_gate), (w_up_hbm, w_up), (w_down_hbm, w_down))
        )
    ]
    for copy in weight_copies:
        copy.start()

    def peer(i):
        return lax.rem(c + i // ep_count, ctx_count), lax.rem(e + lax.rem(i, ep_count), ep_count)

    barrier = pltpu.get_barrier_semaphore()

    def greet(i, carry):
        pl.semaphore_signal(barrier, inc=1, device_id=peer(i), device_id_type=MESH)
        return carry

    lax.fori_loop(1, devices, greet, 0)
    pl.semaphore_wait(barrier, devices - 1)

    kv_copies = [
        pltpu.make_async_remote_copy(
            src_ref=ref,
            dst_ref=kv_prev.at[i],
            send_sem=kv_send.at[i],
            recv_sem=kv_recv.at[i],
            device_id=(lax.rem(c + 1, ctx_count), e),
            device_id_type=MESH,
        )
        for i, ref in enumerate((k_ref, v_ref))
    ]
    for copy in kv_copies:
        copy.start()

    named = jnp.zeros((ep_count * block, tokens), f32)
    for j in range(ids_t_ref.shape[0]):
        named += jnp.where(ids_t_ref[j : j + 1, :] == row_meta_ref[:, 0:1], 1.0, 0.0)
    count = jnp.dot(named.astype(bf16), upper_ref[...], preferred_element_type=f32)
    taken = jnp.where(count.astype(jnp.int32) == row_meta_ref[:, 2:3] + 1, named, 0.0)
    for k in range(chunks):
        tall[:, k * tokens : (k + 1) * tokens] = jnp.where(
            row_meta_ref[:, 1:2] == k, taken, 0.0
        ).astype(bf16)

    query_pos = c * tokens + lax.broadcasted_iota(jnp.int32, (tokens, 2 * tokens), 0)
    key_pos = (c - 1) * tokens + lax.broadcasted_iota(jnp.int32, (tokens, 2 * tokens), 1)
    first_pos = jnp.zeros((tokens, 2 * tokens), jnp.int32)
    start = jnp.int32(0)
    for i in range(lengths_ref.shape[1]):
        first_pos = jnp.where(query_pos >= start, start, first_pos)
        start = start + lengths_ref[0, i]
    visible = (key_pos <= query_pos) & (key_pos >= first_pos)
    score_scale = 1.0 / math.sqrt(HEAD_SIZE)

    for copy in kv_copies:
        copy.wait()

    for kv in range(KEY_VALUE_HEADS):
        kv_cols = slice(kv * HEAD_SIZE, (kv + 1) * HEAD_SIZE)
        keys = jnp.concatenate([kv_prev[0, :, kv_cols], k_ref[:, kv_cols]], axis=0)
        values = jnp.concatenate([kv_prev[1, :, kv_cols], v_ref[:, kv_cols]], axis=0)

        def attend(h, carry, kv=kv, keys=keys, values=values):
            for one in range(4):
                head = kv * head_groups + h * 4 + one
                cols = pl.ds(pl.multiple_of(head * HEAD_SIZE, HEAD_SIZE), HEAD_SIZE)
                scores = lax.dot_general(
                    q_ref[:, cols], keys, (((1,), (1,)), ((), ())), preferred_element_type=f32
                )
                scores = jnp.where(visible, scores * score_scale, -1e30)
                top = jnp.max(scores, axis=-1, keepdims=True)
                weights = jnp.where(visible, jnp.exp(scores - top), 0.0)
                total = jnp.sum(weights, axis=-1, keepdims=True)
                summed = jnp.dot(weights.astype(bf16), values, preferred_element_type=f32)
                context[:, cols] = summed / total
            return carry

        lax.fori_loop(0, head_groups // 4, attend, 0)

    def add_square(h, running):
        part = context[:, pl.ds(pl.multiple_of(h * HEAD_SIZE, HEAD_SIZE), HEAD_SIZE)]
        return running + part * part

    squares = lax.fori_loop(0, QUERY_HEADS, add_square, jnp.zeros((tokens, HEAD_SIZE), f32))
    inverse = lax.rsqrt(jnp.sum(squares, axis=-1, keepdims=True) * (1.0 / D) + 1e-06)
    for cc in range(ctx_count):
        for k in range(chunks):
            cols = slice(cc * wide + k * LANES, cc * wide + (k + 1) * LANES)
            normed[k * tokens : (k + 1) * tokens, cc * LANES : (cc + 1) * LANES] = (
                context[:, cols] * inverse * gain_ref[:, cols].astype(f32)
            ).astype(bf16)

    placed = jnp.dot(tall[...], normed[...], preferred_element_type=f32).astype(bf16)
    for cc in range(ctx_count):
        sent_rows[cc] = placed[:, cc * LANES : (cc + 1) * LANES]

    me = c * ep_count + e

    def rows_at(ref, cc, ee):
        return ref.at[cc, pl.ds(pl.multiple_of(ee * block, 16), block), :]

    def exchange(i, source, target, send_sem, recv_sem):
        cc, ee = peer(i)
        return pltpu.make_async_remote_copy(
            src_ref=rows_at(source, cc, ee),
            dst_ref=rows_at(target, c, e),
            send_sem=send_sem.at[i],
            recv_sem=recv_sem.at[me],
            device_id=(cc, ee),
            device_id_type=MESH,
        )

    def arrival(i, source, target, send_sem, recv_sem):
        cc, ee = peer(i)
        return pltpu.make_async_remote_copy(
            src_ref=rows_at(source, cc, ee),
            dst_ref=rows_at(target, cc, ee),
            send_sem=send_sem.at[i],
            recv_sem=recv_sem.at[cc * ep_count + ee],
            device_id=(cc, ee),
            device_id_type=MESH,
        )

    def all_exchange(source, target, send_sem, recv_sem):
        def begin(i, carry):
            exchange(i, source, target, send_sem, recv_sem).start()
            return carry

        lax.fori_loop(1, devices, begin, 0)
        own = pl.ds(pl.multiple_of(e * block, 16), block)
        target[c, own, :] = source[c, own, :]

        def end(i, carry):
            arrival(i, source, target, send_sem, recv_sem).wait_recv()
            return carry

        lax.fori_loop(1, devices, end, 0)

    def all_sent(source, target, send_sem, recv_sem):
        def end(i, carry):
            exchange(i, source, target, send_sem, recv_sem).wait_send()
            return carry

        lax.fori_loop(1, devices, end, 0)

    def unturned(ref):
        cat = jnp.concatenate([ref[cc] for cc in range(ctx_count)], axis=1)
        return jnp.dot(perm_ref[...], cat, preferred_element_type=f32).astype(bf16)

    all_exchange(sent_rows, got_rows, rows_send, rows_recv)
    ordered = unturned(got_rows)
    for cc in range(ctx_count):
        for k in range(chunks):
            flat[cc * slots : (cc + 1) * slots, k * LANES : (k + 1) * LANES] = ordered[
                k * slots : (k + 1) * slots, cc * LANES : (cc + 1) * LANES
            ]

    weight_copies[0].wait()
    weight_copies[1].wait()
    others = [lax.rem(c + d, ctx_count) for d in range(1, ctx_count)]

    def part_copy(j, d, cc, slot):
        return pltpu.make_async_remote_copy(
            src_ref=partial.at[j, cc],
            dst_ref=got_partial.at[j, slot],
            send_sem=part_send.at[j, d],
            recv_sem=part_recv.at[j, slot],
            device_id=(cc, e),
            device_id_type=MESH,
        )

    def hid_copy(j, d, cc, slot):
        return pltpu.make_async_remote_copy(
            src_ref=hidden.at[j],
            dst_ref=got_hidden.at[j, slot],
            send_sem=hid_send.at[j, d],
            recv_sem=hid_recv.at[j, slot],
            device_id=(cc, e),
            device_id_type=MESH,
        )

    for j in range(PIECES):
        cols = slice(j * piece, (j + 1) * piece)
        gate = jnp.dot(flat[...], w_gate[:, cols], preferred_element_type=f32).astype(bf16)
        up = jnp.dot(flat[...], w_up[:, cols], preferred_element_type=f32).astype(bf16)
        for cc in range(ctx_count):
            partial[j, cc, :, 0:piece] = gate[cc * slots : (cc + 1) * slots]
            partial[j, cc, :, piece : 2 * piece] = up[cc * slots : (cc + 1) * slots]
        for d, cc in enumerate(others):
            part_copy(j, d, cc, c).start()

    for j in range(PIECES):
        proj = partial[j, c].astype(f32)
        for d, cc in enumerate(others):
            part_copy(j, d, cc, cc).wait_recv()
            proj += got_partial[j, cc].astype(f32)
        gate, up = proj[:, 0:piece], proj[:, piece : 2 * piece]
        hidden[j] = (gate / (1.0 + jnp.exp(-gate)) * up).astype(bf16)
        for d, cc in enumerate(others):
            hid_copy(j, d, cc, c).start()
        got_hidden[j, c] = hidden[j]

    weight_copies[2].wait()
    down = jnp.zeros((ctx_count * slots, wide), f32)
    for j in range(PIECES):
        for d, cc in enumerate(others):
            hid_copy(j, d, cc, cc).wait_recv()
        rows = jnp.concatenate([got_hidden[j, cc] for cc in range(ctx_count)], axis=0)
        down += jnp.dot(
            rows, w_down[j * piece : (j + 1) * piece, :], preferred_element_type=f32
        )
    down = down.astype(bf16)
    for cc in range(ctx_count):
        for k in range(chunks):
            turned[k * slots : (k + 1) * slots, cc * LANES : (cc + 1) * LANES] = down[
                cc * slots : (cc + 1) * slots, k * LANES : (k + 1) * LANES
            ]
    back = jnp.dot(perm_t_ref[...], turned[...], preferred_element_type=f32).astype(bf16)
    for cc in range(ctx_count):
        sent_out[cc] = back[:, cc * LANES : (cc + 1) * LANES]
    all_exchange(sent_out, got_out, out_send, out_recv)
    ordered = unturned(got_out)
    for cc in range(ctx_count):
        for k in range(chunks):
            cols = slice(cc * wide + k * LANES, cc * wide + (k + 1) * LANES)
            expert_out[:, cols] = ordered[k * slots : (k + 1) * slots, cc * LANES : (cc + 1) * LANES]

    hits = jnp.zeros((tokens, slots), f32)
    mix = jnp.zeros((tokens, slots), f32)
    for j in range(ids_ref.shape[1]):
        hit = ids_ref[:, j : j + 1] == col_meta_ref[0:1, :]
        hits += jnp.where(hit, 1.0, 0.0)
        mix += jnp.where(hit, gates_ref[:, j : j + 1], 0.0)
    count = jnp.dot(lower_ref[...], hits.astype(bf16), preferred_element_type=f32)
    mix = jnp.where(count.astype(jnp.int32) == col_meta_ref[1:2, :] + 1, mix, 0.0)
    high = mix.astype(bf16)
    low = (mix - high.astype(f32)).astype(bf16)
    both = jnp.concatenate([high, low], axis=0)
    for cc in range(ctx_count):
        cols = slice(cc * wide, (cc + 1) * wide)
        mixed = jnp.dot(both, expert_out[:, cols], preferred_element_type=f32)
        out_ref[:, cols] = (context[:, cols] + mixed[0:tokens] + mixed[tokens:]).astype(bf16)

    for copy_set in (
        (sent_rows, got_rows, rows_send, rows_recv),
        (sent_out, got_out, out_send, out_recv),
    ):
        all_sent(*copy_set)
    for j in range(PIECES):
        for d, cc in enumerate(others):
            part_copy(j, d, cc, c).wait_send()
            hid_copy(j, d, cc, c).wait_send()


def local_fused(
    queries,
    key_heads,
    value_head_array,
    trace_lengths,
    expert_ids,
    gate_weights,
    norm_gain,
    w_gate,
    w_up,
    w_down,
):
    bf16 = jnp.bfloat16
    ctx_count, ep_count = lax.axis_size("ctx"), lax.axis_size("ep")
    tokens = queries.shape[1]
    wide, units = w_gate.shape
    chunks = wide // LANES
    slots = ep_count * CAP
    tall_rows = chunks * slots
    n = np.arange(tall_rows)
    row_e, row_k, row_s = n // (chunks * CAP), n // CAP % chunks, n % CAP
    row_meta = np.stack([row_e, row_k, row_s], axis=1).astype(np.int32)
    m = np.arange(slots)
    col_meta = np.stack([m // CAP, m % CAP], axis=0).astype(np.int32)
    lower = np.tril(np.ones((tokens, tokens), np.float32))
    perm = np.zeros((tall_rows, tall_rows), np.float32)
    perm[row_k * slots + row_e * CAP + row_s, n] = 1.0
    vmem = pl.BlockSpec(memory_space=pltpu.VMEM)
    anywhere = pl.BlockSpec(memory_space=pl.ANY)
    dma = pltpu.SemaphoreType.DMA
    devices = ctx_count * ep_count
    piece = units // PIECES
    across = ctx_count * LANES
    out = pl.pallas_call(
        functools.partial(fused, ctx_count, ep_count),
        out_shape=jax.ShapeDtypeStruct((tokens, D), bf16),
        in_specs=[vmem] * 3
        + [pl.BlockSpec(memory_space=pltpu.SMEM)]
        + [vmem] * 10
        + [anywhere] * 3,
        out_specs=vmem,
        scratch_shapes=[
            pltpu.VMEM((2, tokens, KEY_VALUE_HEADS * HEAD_SIZE), bf16),
            pltpu.VMEM((tokens, D), jnp.float32),
            pltpu.VMEM((chunks * tokens, across), bf16),
            pltpu.VMEM((tall_rows, chunks * tokens), bf16),
            pltpu.VMEM((ctx_count, tall_rows, LANES), bf16),
            pltpu.VMEM((ctx_count, tall_rows, LANES), bf16),
            pltpu.VMEM((ctx_count * slots, wide), bf16),
            pltpu.VMEM((PIECES, ctx_count, slots, 2 * piece), bf16),
            pltpu.VMEM((PIECES, ctx_count, slots, 2 * piece), bf16),
            pltpu.VMEM((PIECES, slots, piece), bf16),
            pltpu.VMEM((PIECES, ctx_count, slots, piece), bf16),
            pltpu.VMEM((tall_rows, across), bf16),
            pltpu.VMEM((ctx_count, tall_rows, LANES), bf16),
            pltpu.VMEM((ctx_count, tall_rows, LANES), bf16),
            pltpu.VMEM((slots, D), bf16),
            pltpu.VMEM((wide, units), bf16),
            pltpu.VMEM((wide, units), bf16),
            pltpu.VMEM((units, wide), bf16),
            dma((3,)),
            dma((2,)),
            dma((2,)),
            dma((devices,)),
            dma((devices,)),
            dma((PIECES, ctx_count)),
            dma((PIECES, ctx_count)),
            dma((PIECES, ctx_count)),
            dma((PIECES, ctx_count)),
            dma((devices,)),
            dma((devices,)),
        ],
        compiler_params=pltpu.CompilerParams(
            collective_id=0, has_side_effects=True, vmem_limit_bytes=56 * 1024 * 1024
        ),
        cost_estimate=pl.CostEstimate(
            flops=4_000_000_000, bytes_accessed=14_000_000, transcendentals=1_000_000
        ),
    )(
        expert_ids[0],
        expert_ids[0].T,
        gate_weights[0],
        trace_lengths,
        queries[0],
        key_heads[0],
        value_head_array[0],
        norm_gain[None],
        row_meta,
        col_meta,
        lower.astype(bf16),
        lower.T.astype(bf16),
        perm.astype(bf16),
        perm.T.astype(bf16),
        w_gate,
        w_up,
        w_down,
    )
    return out[None]


def local(*args):
    ctx_count, ep_count = lax.axis_size("ctx"), lax.axis_size("ep")
    wide, units = args[7].shape
    aligned = (wide // LANES * CAP) % 16 == 0 and units % (PIECES * LANES) == 0
    if ep_count == EXP_WIN and ctx_count == 4 and aligned:
        return local_fused(*args)
    return local_plain(*args)


def solution(mesh):
    in_specs = (
        P("ep", "ctx", None),
        P("ep", "ctx", None),
        P("ep", "ctx", None),
        P("ep", None),
        P("ep", "ctx", None),
        P("ep", "ctx", None),
        P(),
        P("ctx", "ep"),
        P("ctx", "ep"),
        P("ep", "ctx"),
    )
    out_specs = P("ep", "ctx", None)
    return jax.shard_map(local, mesh=mesh, in_specs=in_specs, out_specs=out_specs, check_vma=False)
```

```python
import functools
import math

import jax
import jax.numpy as jnp
import numpy as np
from jax import lax
from jax.experimental import pallas as pl
from jax.experimental.pallas import tpu as pltpu
from jax.sharding import PartitionSpec as P

D = 4096
HEAD_SIZE = 128
QUERY_HEADS = 32
KEY_VALUE_HEADS = 2
EXP_WIN = 8
CAP = 10


def shifted(block, axis, distance):
    devices = range(lax.axis_size(axis))
    route = [(i - distance, i) for i in devices if i - distance in devices]
    return lax.ppermute(block, axis, route)


def trace_first(trace_lengths, positions):
    trace_ends = jnp.cumsum(trace_lengths)
    starts = trace_ends - trace_lengths
    return jnp.max(jnp.where(starts[None, :] <= positions[:, None], starts[None, :], 0), axis=1)


def experts(stacked, w_gate, w_up, w_down):
    ep_count = lax.axis_size("ep")
    ctx_count = lax.axis_size("ctx")
    slab_size = ep_count // EXP_WIN
    wide = w_gate.shape[0]
    rows = ep_count * CAP
    outgoing = jnp.repeat(stacked, slab_size, axis=0)
    arrived = lax.all_to_all(outgoing, "ep", split_axis=0, concat_axis=0, tiled=True)
    cut = arrived.reshape(rows, ctx_count, wide).transpose(1, 0, 2)
    cut = lax.all_to_all(cut, "ctx", split_axis=0, concat_axis=0, tiled=True)
    flat = cut.reshape(ctx_count * rows, wide)
    gate_part = jnp.dot(flat, w_gate, preferred_element_type=jnp.float32).astype(jnp.bfloat16)
    up_part = jnp.dot(flat, w_up, preferred_element_type=jnp.float32).astype(jnp.bfloat16)
    both = jnp.stack([gate_part, up_part]).reshape(2, ctx_count, rows, -1)
    both = lax.all_to_all(both, "ctx", split_axis=1, concat_axis=1, tiled=True)
    proj = jnp.sum(both.astype(jnp.float32), axis=1)
    hidden = (jax.nn.silu(proj[0]) * proj[1]).astype(jnp.bfloat16)
    hidden = lax.all_gather(hidden, "ctx", axis=0, tiled=True)
    out = jnp.dot(hidden, w_down, preferred_element_type=jnp.float32).astype(jnp.bfloat16)
    out = lax.all_to_all(
        out.reshape(ctx_count, rows, wide), "ctx", split_axis=0, concat_axis=0, tiled=True
    )
    out = out.transpose(1, 0, 2).reshape(ep_count, CAP, ctx_count * wide)
    returned = lax.all_to_all(out, "ep", split_axis=0, concat_axis=0, tiled=True)
    return returned.astype(jnp.float32).reshape(EXP_WIN, slab_size, CAP, D).sum(axis=1)


def local_plain(
    queries,
    key_heads,
    value_head_array,
    trace_lengths,
    expert_ids,
    gate_weights,
    norm_gain,
    w_gate,
    w_up,
    w_down,
):
    rows_per_shard = queries.shape[1]
    head_groups = QUERY_HEADS // KEY_VALUE_HEADS
    ctx_place = lax.axis_index("ctx")
    ctx_count = lax.axis_size("ctx")
    reach_count = ctx_count // 4
    query_pos = ctx_place * rows_per_shard + jnp.arange(rows_per_shard, dtype=jnp.int32)
    first_pos = trace_first(trace_lengths[0], query_pos)
    query_division = queries[0].reshape(rows_per_shard, KEY_VALUE_HEADS, head_groups, HEAD_SIZE)
    score_scale = 1.0 / math.sqrt(HEAD_SIZE)

    def attend(running, kv_piece, offset):
        key_portion, value_portion = kv_piece
        width = key_portion.shape[1]
        size_value = min(512, width)
        old_max, old_total, old_sum = running
        key_division = key_portion[0, 0:size_value].reshape(size_value, KEY_VALUE_HEADS, HEAD_SIZE)
        value_division = value_portion[0, 0:size_value].reshape(
            size_value, KEY_VALUE_HEADS, HEAD_SIZE
        )
        scores = (
            jnp.einsum(
                "tkgd,skd->kgts", query_division, key_division, preferred_element_type=jnp.float32
            )
            * score_scale
        )
        key_pos = offset + 0 + jnp.arange(size_value, dtype=jnp.int32)
        visible = (key_pos[None, :] <= query_pos[:, None]) & (
            key_pos[None, :] >= first_pos[:, None]
        )
        scores = jnp.where(visible, scores, -1e30)
        new_max = jnp.maximum(old_max, jnp.max(scores, axis=-1))
        weights = jnp.where(visible, jnp.exp(scores - new_max[..., None]), 0.0)
        rescale = jnp.exp(old_max - new_max)
        new_total = old_total * rescale + jnp.sum(weights, axis=-1)
        new_sum = old_sum * rescale[..., None] + jnp.einsum(
            "kgts,skd->kgtd",
            weights.astype(jnp.bfloat16),
            value_division,
            preferred_element_type=jnp.float32,
        )
        running = (new_max, new_total, new_sum)
        return running

    empty_state = (
        jnp.full((KEY_VALUE_HEADS, head_groups, rows_per_shard), -1e30, jnp.float32),
        jnp.zeros((KEY_VALUE_HEADS, head_groups, rows_per_shard), jnp.float32),
        jnp.zeros((KEY_VALUE_HEADS, head_groups, rows_per_shard, HEAD_SIZE), jnp.float32),
    )
    own_pair = jnp.stack([key_heads, value_head_array])
    own_state = attend(empty_state, (key_heads, value_head_array), ctx_place * rows_per_shard)

    def earlier_step(i, state):
        moving, running = state
        moving = shifted(moving, "ctx", 1)
        running = attend(running, (moving[0], moving[1]), (ctx_place - i - 1) * rows_per_shard)
        return (moving, running)

    final_state = lax.fori_loop(0, reach_count, earlier_step, (own_pair, own_state))[1]
    context = (
        (final_state[2] / final_state[1][..., None])
        .transpose(2, 0, 1, 3)
        .reshape(rows_per_shard, QUERY_HEADS * HEAD_SIZE)
    )
    mean_square = jnp.mean(context * context, axis=-1, keepdims=True)
    normed = (context * lax.rsqrt(mean_square + 1e-06) * norm_gain.astype(jnp.float32)).astype(
        jnp.bfloat16
    )
    chosen_ids = expert_ids[0]
    weight_rows = gate_weights[0]
    slot_range = jnp.arange(CAP, dtype=jnp.int32)
    placing_list = []
    mixing_list = []
    for e in range(EXP_WIN):
        chosen = chosen_ids == e
        routed = jnp.any(chosen, axis=-1)
        gate_value = jnp.sum(jnp.where(chosen, weight_rows, 0.0), axis=-1)
        slot_index = jnp.cumsum(routed.astype(jnp.int32)) - 1
        taken = (slot_index[None, :] == slot_range[:, None]) & routed[None, :]
        placing_list.append(taken.astype(jnp.bfloat16))
        mixing_list.append(jnp.where(taken.T, gate_value[:, None], 0.0))
    placing = jnp.concatenate(placing_list, axis=0)
    mixing = jnp.concatenate(mixing_list, axis=1)
    stacked = (
        jnp.dot(placing, normed, preferred_element_type=jnp.float32)
        .astype(jnp.bfloat16)
        .reshape(EXP_WIN, CAP, D)
    )
    expert_out = experts(stacked, w_gate, w_up, w_down)
    expert_mix = jnp.dot(
        mixing,
        expert_out.reshape(EXP_WIN * CAP, D),
        precision=lax.Precision.HIGHEST,
        preferred_element_type=jnp.float32,
    )
    return (context + expert_mix).astype(jnp.bfloat16)[None]


LANES = 128
PIECES = 2
SLOT_GROUPS = (6, 4)
MESH = pl.DeviceIdType.MESH


def fused(
    ctx_count,
    ep_count,
    ids_ref,
    gates_ref,
    lengths_ref,
    q_ref,
    k_ref,
    v_ref,
    gain_ref,
    row_meta_ref,
    slot_meta_ref,
    upper_ref,
    perm_a_ref,
    perm_b_ref,
    perm_t_a_ref,
    perm_t_b_ref,
    w_gate_hbm,
    w_up_hbm,
    w_down_hbm,
    out_ref,
    kv_prev,
    context,
    normed,
    tall,
    sent_rows,
    got_rows,
    flat,
    partial,
    got_partial,
    hidden,
    got_hidden,
    turned,
    sent_out,
    got_out,
    expert_out,
    mix,
    w_gate,
    w_up,
    w_down,
    w_sem,
    kv_send,
    kv_recv,
    rows_send,
    rows_recv,
    part_send,
    part_recv,
    hid_send,
    hid_recv,
    out_send,
    out_recv,
):
    f32, bf16 = jnp.float32, jnp.bfloat16
    c = lax.axis_index("ctx")
    e = lax.axis_index("ep")
    devices = ctx_count * ep_count
    tokens = q_ref.shape[0]
    wide = w_gate.shape[0]
    units = w_gate.shape[1]
    chunks = wide // LANES
    slots = ep_count * CAP
    piece = units // PIECES
    head_groups = QUERY_HEADS // KEY_VALUE_HEADS
    groups = range(len(SLOT_GROUPS))
    perms = (perm_a_ref, perm_b_ref)
    perms_t = (perm_t_a_ref, perm_t_b_ref)
    blocks = [chunks * size for size in SLOT_GROUPS]
    bases = [ep_count * chunks * sum(SLOT_GROUPS[:g]) for g in groups]
    slot_counts = [ep_count * size for size in SLOT_GROUPS]
    slot_bases = [ep_count * sum(SLOT_GROUPS[:g]) for g in groups]

    weight_copies = [
        pltpu.make_async_copy(hbm, vmem, w_sem.at[i])
        for i, (hbm, vmem) in enumerate(
            ((w_gate_hbm, w_gate), (w_up_hbm, w_up), (w_down_hbm, w_down))
        )
    ]
    for copy in weight_copies:
        copy.start()

    def peer(i):
        return lax.rem(c + i // ep_count, ctx_count), lax.rem(e + lax.rem(i, ep_count), ep_count)

    barrier = pltpu.get_barrier_semaphore()

    def greet(i, carry):
        pl.semaphore_signal(barrier, inc=1, device_id=peer(i), device_id_type=MESH)
        return carry

    lax.fori_loop(1, devices, greet, 0)
    named = jnp.zeros((chunks * slots, tokens), f32)
    for j in range(ids_ref.shape[0]):
        named += jnp.where(ids_ref[j : j + 1, :] == row_meta_ref[:, 0:1], 1.0, 0.0)
    count = jnp.dot(named.astype(bf16), upper_ref[...], preferred_element_type=f32)
    taken = jnp.where(count.astype(jnp.int32) == row_meta_ref[:, 2:3] + 1, named, 0.0)
    for k in range(chunks):
        tall[:, k * tokens : (k + 1) * tokens] = jnp.where(
            row_meta_ref[:, 1:2] == k, taken, 0.0
        ).astype(bf16)

    pl.semaphore_wait(barrier, devices - 1)

    kv_copies = [
        pltpu.make_async_remote_copy(
            src_ref=ref,
            dst_ref=kv_prev.at[i],
            send_sem=kv_send.at[i],
            recv_sem=kv_recv.at[i],
            device_id=(lax.rem(c + 1, ctx_count), e),
            device_id_type=MESH,
        )
        for i, ref in enumerate((k_ref, v_ref))
    ]
    for copy in kv_copies:
        copy.start()

    hits = jnp.zeros((slots, tokens), f32)
    gate_at = jnp.zeros((slots, tokens), f32)
    for j in range(ids_ref.shape[0]):
        hit = ids_ref[j : j + 1, :] == slot_meta_ref[:, 0:1]
        hits += jnp.where(hit, 1.0, 0.0)
        gate_at += jnp.where(hit, gates_ref[j : j + 1, :], 0.0)
    count = jnp.dot(hits.astype(bf16), upper_ref[...], preferred_element_type=f32)
    gate_at = jnp.where(count.astype(jnp.int32) == slot_meta_ref[:, 1:2] + 1, gate_at, 0.0)
    high = gate_at.astype(bf16)
    mix[:, 0:tokens] = high
    mix[:, tokens : 2 * tokens] = (gate_at - high.astype(f32)).astype(bf16)

    query_pos = c * tokens + lax.broadcasted_iota(jnp.int32, (tokens, 2 * tokens), 0)
    key_pos = (c - 1) * tokens + lax.broadcasted_iota(jnp.int32, (tokens, 2 * tokens), 1)
    first_pos = jnp.zeros((tokens, 2 * tokens), jnp.int32)
    start = jnp.int32(0)
    for i in range(lengths_ref.shape[1]):
        first_pos = jnp.where(query_pos >= start, start, first_pos)
        start = start + lengths_ref[0, i]
    visible = (key_pos <= query_pos) & (key_pos >= first_pos)
    score_scale = 1.0 / math.sqrt(HEAD_SIZE)

    for copy in kv_copies:
        copy.wait()

    for kv in range(KEY_VALUE_HEADS):
        kv_cols = slice(kv * HEAD_SIZE, (kv + 1) * HEAD_SIZE)
        keys = jnp.concatenate([kv_prev[0, :, kv_cols], k_ref[:, kv_cols]], axis=0)
        values = jnp.concatenate([kv_prev[1, :, kv_cols], v_ref[:, kv_cols]], axis=0)

        def attend(h, carry, kv=kv, keys=keys, values=values):
            for one in range(4):
                head = kv * head_groups + h * 4 + one
                cols = pl.ds(pl.multiple_of(head * HEAD_SIZE, HEAD_SIZE), HEAD_SIZE)
                scores = lax.dot_general(
                    q_ref[:, cols], keys, (((1,), (1,)), ((), ())), preferred_element_type=f32
                )
                scores = jnp.where(visible, scores * score_scale, -1e30)
                top = jnp.max(scores, axis=-1, keepdims=True)
                weights = jnp.where(visible, jnp.exp(scores - top), 0.0)
                total = jnp.sum(weights, axis=-1, keepdims=True)
                summed = jnp.dot(weights.astype(bf16), values, preferred_element_type=f32)
                context[:, cols] = summed / total
            return carry

        lax.fori_loop(0, head_groups // 4, attend, 0)

    def add_square(h, running):
        part = context[:, pl.ds(pl.multiple_of(h * HEAD_SIZE, HEAD_SIZE), HEAD_SIZE)]
        return running + part * part

    squares = lax.fori_loop(0, QUERY_HEADS, add_square, jnp.zeros((tokens, HEAD_SIZE), f32))
    inverse = lax.rsqrt(jnp.sum(squares, axis=-1, keepdims=True) * (1.0 / D) + 1e-06)
    for cc in range(ctx_count):
        for k in range(chunks):
            cols = slice(cc * wide + k * LANES, cc * wide + (k + 1) * LANES)
            normed[k * tokens : (k + 1) * tokens, cc * LANES : (cc + 1) * LANES] = (
                context[:, cols] * inverse * gain_ref[:, cols].astype(f32)
            ).astype(bf16)

    me = c * ep_count + e

    def rows_at(ref, g, cc, ee):
        return ref.at[cc, pl.ds(pl.multiple_of(bases[g] + ee * blocks[g], 16), blocks[g]), :]

    def exchange(g, i, source, target, send_sem, recv_sem):
        cc, ee = peer(i)
        return pltpu.make_async_remote_copy(
            src_ref=rows_at(source, g, cc, ee),
            dst_ref=rows_at(target, g, c, e),
            send_sem=send_sem.at[g, i],
            recv_sem=recv_sem.at[g, me],
            device_id=(cc, ee),
            device_id_type=MESH,
        )

    def arrival(g, i, source, target, send_sem, recv_sem):
        cc, ee = peer(i)
        return pltpu.make_async_remote_copy(
            src_ref=rows_at(source, g, cc, ee),
            dst_ref=rows_at(target, g, cc, ee),
            send_sem=send_sem.at[g, i],
            recv_sem=recv_sem.at[g, cc * ep_count + ee],
            device_id=(cc, ee),
            device_id_type=MESH,
        )

    def send_all(g, source, target, send_sem, recv_sem):
        def begin(i, carry):
            exchange(g, i, source, target, send_sem, recv_sem).start()
            return carry

        lax.fori_loop(1, devices, begin, 0)
        own = pl.ds(pl.multiple_of(bases[g] + e * blocks[g], 16), blocks[g])
        target[c, own, :] = source[c, own, :]

    def receive_all(g, source, target, send_sem, recv_sem):
        def end(i, carry):
            arrival(g, i, source, target, send_sem, recv_sem).wait_recv()
            return carry

        lax.fori_loop(1, devices, end, 0)

    def all_sent(g, source, target, send_sem, recv_sem):
        def end(i, carry):
            exchange(g, i, source, target, send_sem, recv_sem).wait_send()
            return carry

        lax.fori_loop(1, devices, end, 0)

    def unturned(g, ref):
        rows = slice(bases[g], bases[g] + ep_count * blocks[g])
        cat = jnp.concatenate([ref[cc, rows, :] for cc in range(ctx_count)], axis=1)
        return jnp.dot(perms[g][...], cat, preferred_element_type=f32).astype(bf16)

    row_set = (sent_rows, got_rows, rows_send, rows_recv)
    out_set = (sent_out, got_out, out_send, out_recv)
    others = [lax.rem(c + d, ctx_count) for d in range(1, ctx_count)]

    def part_copy(g, j, d, cc, slot):
        rows = pl.ds(slot_bases[g], slot_counts[g])
        return pltpu.make_async_remote_copy(
            src_ref=partial.at[j, cc, rows, :],
            dst_ref=got_partial.at[j, slot, rows, :],
            send_sem=part_send.at[g, j, d],
            recv_sem=part_recv.at[g, j, slot],
            device_id=(cc, e),
            device_id_type=MESH,
        )

    def hid_copy(g, j, d, cc, slot):
        rows = pl.ds(slot_bases[g], slot_counts[g])
        return pltpu.make_async_remote_copy(
            src_ref=hidden.at[j, rows, :],
            dst_ref=got_hidden.at[j, slot, rows, :],
            send_sem=hid_send.at[g, j, d],
            recv_sem=hid_recv.at[g, j, slot],
            device_id=(cc, e),
            device_id_type=MESH,
        )

    def begin_rows(g):
        rows = slice(bases[g], bases[g] + ep_count * blocks[g])
        placed = jnp.dot(tall[rows, :], normed[...], preferred_element_type=f32).astype(bf16)
        for cc in range(ctx_count):
            sent_rows[cc, rows, :] = placed[:, cc * LANES : (cc + 1) * LANES]
        send_all(g, *row_set)

    def multiply(g, send):
        receive_all(g, *row_set)
        ordered = unturned(g, got_rows)
        count, base = slot_counts[g], slot_bases[g]
        first = ctx_count * base
        for cc in range(ctx_count):
            for k in range(chunks):
                flat[
                    first + cc * count : first + (cc + 1) * count, k * LANES : (k + 1) * LANES
                ] = ordered[k * count : (k + 1) * count, cc * LANES : (cc + 1) * LANES]
        if g == 0:
            weight_copies[0].wait()
            weight_copies[1].wait()
        rows = flat[first : first + ctx_count * count, :]
        for j in range(PIECES):
            cols = slice(j * piece, (j + 1) * piece)
            gate = jnp.dot(rows, w_gate[:, cols], preferred_element_type=f32).astype(bf16)
            up = jnp.dot(rows, w_up[:, cols], preferred_element_type=f32).astype(bf16)
            for cc in range(ctx_count):
                here = slice(cc * count, (cc + 1) * count)
                partial[j, cc, base : base + count, 0:piece] = gate[here]
                partial[j, cc, base : base + count, piece : 2 * piece] = up[here]
            if send:
                send_partial(g, j)

    def send_partial(g, j):
        for d, cc in enumerate(others):
            part_copy(g, j, d, cc, c).start()

    def activate(g):
        rows = pl.ds(slot_bases[g], slot_counts[g])
        for j in range(PIECES):
            proj = partial[j, c, rows, :].astype(f32)
            for d, cc in enumerate(others):
                part_copy(g, j, d, cc, cc).wait_recv()
                proj += got_partial[j, cc, rows, :].astype(f32)
            gate, up = proj[:, 0:piece], proj[:, piece : 2 * piece]
            units_here = (gate / (1.0 + jnp.exp(-gate)) * up).astype(bf16)
            hidden[j, rows, :] = units_here
            for d, cc in enumerate(others):
                hid_copy(g, j, d, cc, c).start()
            got_hidden[j, c, rows, :] = units_here

    def project_down(g):
        count, base = slot_counts[g], slot_bases[g]
        if g == 0:
            weight_copies[2].wait()
        down = jnp.zeros((ctx_count * count, wide), f32)
        for j in range(PIECES):
            for d, cc in enumerate(others):
                hid_copy(g, j, d, cc, cc).wait_recv()
            rows = jnp.concatenate(
                [got_hidden[j, cc, base : base + count, :] for cc in range(ctx_count)], axis=0
            )
            down += jnp.dot(
                rows, w_down[j * piece : (j + 1) * piece, :], preferred_element_type=f32
            )
        down = down.astype(bf16)
        rows = slice(bases[g], bases[g] + ep_count * blocks[g])
        for cc in range(ctx_count):
            for k in range(chunks):
                turned[
                    bases[g] + k * count : bases[g] + (k + 1) * count,
                    cc * LANES : (cc + 1) * LANES,
                ] = down[cc * count : (cc + 1) * count, k * LANES : (k + 1) * LANES]
        back = jnp.dot(perms_t[g][...], turned[rows, :], preferred_element_type=f32).astype(bf16)
        for cc in range(ctx_count):
            sent_out[cc, rows, :] = back[:, cc * LANES : (cc + 1) * LANES]
        send_all(g, *out_set)

    def take_back(g):
        receive_all(g, *out_set)
        ordered = unturned(g, got_out)
        count, base = slot_counts[g], slot_bases[g]
        for cc in range(ctx_count):
            for k in range(chunks):
                cols = slice(cc * wide + k * LANES, cc * wide + (k + 1) * LANES)
                expert_out[base : base + count, cols] = ordered[
                    k * count : (k + 1) * count, cc * LANES : (cc + 1) * LANES
                ]

    begin_rows(0)
    begin_rows(1)
    multiply(0, True)
    multiply(1, False)
    activate(0)
    for j in range(PIECES):
        send_partial(1, j)
    project_down(0)
    activate(1)
    project_down(1)
    take_back(0)
    take_back(1)

    for cc in range(ctx_count):
        cols = slice(cc * wide, (cc + 1) * wide)
        mixed = lax.dot_general(
            mix[...], expert_out[:, cols], (((0,), (0,)), ((), ())), preferred_element_type=f32
        )
        out_ref[:, cols] = (context[:, cols] + mixed[0:tokens] + mixed[tokens:]).astype(bf16)

    for g in groups:
        all_sent(g, *row_set)
        all_sent(g, *out_set)
        for j in range(PIECES):
            for d, cc in enumerate(others):
                part_copy(g, j, d, cc, c).wait_send()
                hid_copy(g, j, d, cc, c).wait_send()


def local_fused(
    queries,
    key_heads,
    value_head_array,
    trace_lengths,
    expert_ids,
    gate_weights,
    norm_gain,
    w_gate,
    w_up,
    w_down,
):
    bf16 = jnp.bfloat16
    ctx_count, ep_count = lax.axis_size("ctx"), lax.axis_size("ep")
    tokens = queries.shape[1]
    wide, units = w_gate.shape
    chunks = wide // LANES
    slots = ep_count * CAP
    tall_rows = chunks * slots
    row_meta, slot_meta, perms = [], [], []
    for g, size in enumerate(SLOT_GROUPS):
        first = sum(SLOT_GROUPS[:g])
        n = np.arange(ep_count * chunks * size)
        row_e, row_k, row_s = n // (chunks * size), n // size % chunks, n % size
        row_meta.append(np.stack([row_e, row_k, row_s + first], axis=1).astype(np.int32))
        m = np.arange(ep_count * size)
        slot_meta.append(np.stack([m // size, m % size + first], axis=1).astype(np.int32))
        perm = np.zeros((n.size, n.size), np.float32)
        perm[(row_k * ep_count + row_e) * size + row_s, n] = 1.0
        perms.append(perm)
    row_meta, slot_meta = np.concatenate(row_meta), np.concatenate(slot_meta)
    upper = np.triu(np.ones((tokens, tokens), np.float32))
    vmem = pl.BlockSpec(memory_space=pltpu.VMEM)
    anywhere = pl.BlockSpec(memory_space=pl.ANY)
    dma = pltpu.SemaphoreType.DMA
    devices = ctx_count * ep_count
    groups = len(SLOT_GROUPS)
    piece = units // PIECES
    across = ctx_count * LANES
    out = pl.pallas_call(
        functools.partial(fused, ctx_count, ep_count),
        out_shape=jax.ShapeDtypeStruct((tokens, D), bf16),
        in_specs=[vmem] * 2
        + [pl.BlockSpec(memory_space=pltpu.SMEM)]
        + [vmem] * 11
        + [anywhere] * 3,
        out_specs=vmem,
        scratch_shapes=[
            pltpu.VMEM((2, tokens, KEY_VALUE_HEADS * HEAD_SIZE), bf16),
            pltpu.VMEM((tokens, D), jnp.float32),
            pltpu.VMEM((chunks * tokens, across), bf16),
            pltpu.VMEM((tall_rows, chunks * tokens), bf16),
            pltpu.VMEM((ctx_count, tall_rows, LANES), bf16),
            pltpu.VMEM((ctx_count, tall_rows, LANES), bf16),
            pltpu.VMEM((ctx_count * slots, wide), bf16),
            pltpu.VMEM((PIECES, ctx_count, slots, 2 * piece), bf16),
            pltpu.VMEM((PIECES, ctx_count, slots, 2 * piece), bf16),
            pltpu.VMEM((PIECES, slots, piece), bf16),
            pltpu.VMEM((PIECES, ctx_count, slots, piece), bf16),
            pltpu.VMEM((tall_rows, across), bf16),
            pltpu.VMEM((ctx_count, tall_rows, LANES), bf16),
            pltpu.VMEM((ctx_count, tall_rows, LANES), bf16),
            pltpu.VMEM((slots, D), bf16),
            pltpu.VMEM((slots, 2 * tokens), bf16),
            pltpu.VMEM((wide, units), bf16),
            pltpu.VMEM((wide, units), bf16),
            pltpu.VMEM((units, wide), bf16),
            dma((3,)),
            dma((2,)),
            dma((2,)),
            dma((groups, devices)),
            dma((groups, devices)),
            dma((groups, PIECES, ctx_count)),
            dma((groups, PIECES, ctx_count)),
            dma((groups, PIECES, ctx_count)),
            dma((groups, PIECES, ctx_count)),
            dma((groups, devices)),
            dma((groups, devices)),
        ],
        compiler_params=pltpu.CompilerParams(
            collective_id=0, has_side_effects=True, vmem_limit_bytes=56 * 1024 * 1024
        ),
        cost_estimate=pl.CostEstimate(
            flops=4_000_000_000, bytes_accessed=14_000_000, transcendentals=1_000_000
        ),
    )(
        expert_ids[0].T,
        gate_weights[0].T,
        trace_lengths,
        queries[0],
        key_heads[0],
        value_head_array[0],
        norm_gain[None],
        row_meta,
        slot_meta,
        upper.astype(bf16),
        perms[0].astype(bf16),
        perms[1].astype(bf16),
        perms[0].T.astype(bf16),
        perms[1].T.astype(bf16),
        w_gate,
        w_up,
        w_down,
    )
    return out[None]


def local(*args):
    ctx_count, ep_count = lax.axis_size("ctx"), lax.axis_size("ep")
    wide, units = args[7].shape
    aligned = all((wide // LANES * size) % 16 == 0 for size in SLOT_GROUPS) and units % (PIECES * LANES) == 0
    if ep_count == EXP_WIN and ctx_count == 4 and aligned:
        return local_fused(*args)
    return local_plain(*args)


def solution(mesh):
    in_specs = (
        P("ep", "ctx", None),
        P("ep", "ctx", None),
        P("ep", "ctx", None),
        P("ep", None),
        P("ep", "ctx", None),
        P("ep", "ctx", None),
        P(),
        P("ctx", "ep"),
        P("ctx", "ep"),
        P("ep", "ctx"),
    )
    out_specs = P("ep", "ctx", None)
    return jax.shard_map(local, mesh=mesh, in_specs=in_specs, out_specs=out_specs, check_vma=False)
```

```python
import functools
import math

import jax
import jax.numpy as jnp
import numpy as np
from jax import lax
from jax.experimental import pallas as pl
from jax.experimental.pallas import tpu as pltpu
from jax.sharding import PartitionSpec as P

D = 4096
HEAD_SIZE = 128
QUERY_HEADS = 32
KEY_VALUE_HEADS = 2
EXP_WIN = 8
CAP = 10


def shifted(block, axis, distance):
    devices = range(lax.axis_size(axis))
    route = [(i - distance, i) for i in devices if i - distance in devices]
    return lax.ppermute(block, axis, route)


def trace_first(trace_lengths, positions):
    trace_ends = jnp.cumsum(trace_lengths)
    starts = trace_ends - trace_lengths
    return jnp.max(jnp.where(starts[None, :] <= positions[:, None], starts[None, :], 0), axis=1)


def experts(stacked, w_gate, w_up, w_down):
    ep_count = lax.axis_size("ep")
    ctx_count = lax.axis_size("ctx")
    slab_size = ep_count // EXP_WIN
    wide = w_gate.shape[0]
    rows = ep_count * CAP
    outgoing = jnp.repeat(stacked, slab_size, axis=0)
    arrived = lax.all_to_all(outgoing, "ep", split_axis=0, concat_axis=0, tiled=True)
    cut = arrived.reshape(rows, ctx_count, wide).transpose(1, 0, 2)
    cut = lax.all_to_all(cut, "ctx", split_axis=0, concat_axis=0, tiled=True)
    flat = cut.reshape(ctx_count * rows, wide)
    gate_part = jnp.dot(flat, w_gate, preferred_element_type=jnp.float32).astype(jnp.bfloat16)
    up_part = jnp.dot(flat, w_up, preferred_element_type=jnp.float32).astype(jnp.bfloat16)
    both = jnp.stack([gate_part, up_part]).reshape(2, ctx_count, rows, -1)
    both = lax.all_to_all(both, "ctx", split_axis=1, concat_axis=1, tiled=True)
    proj = jnp.sum(both.astype(jnp.float32), axis=1)
    hidden = (jax.nn.silu(proj[0]) * proj[1]).astype(jnp.bfloat16)
    hidden = lax.all_gather(hidden, "ctx", axis=0, tiled=True)
    out = jnp.dot(hidden, w_down, preferred_element_type=jnp.float32).astype(jnp.bfloat16)
    out = lax.all_to_all(
        out.reshape(ctx_count, rows, wide), "ctx", split_axis=0, concat_axis=0, tiled=True
    )
    out = out.transpose(1, 0, 2).reshape(ep_count, CAP, ctx_count * wide)
    returned = lax.all_to_all(out, "ep", split_axis=0, concat_axis=0, tiled=True)
    return returned.astype(jnp.float32).reshape(EXP_WIN, slab_size, CAP, D).sum(axis=1)


def local_plain(
    queries,
    key_heads,
    value_head_array,
    trace_lengths,
    expert_ids,
    gate_weights,
    norm_gain,
    w_gate,
    w_up,
    w_down,
):
    rows_per_shard = queries.shape[1]
    head_groups = QUERY_HEADS // KEY_VALUE_HEADS
    ctx_place = lax.axis_index("ctx")
    ctx_count = lax.axis_size("ctx")
    reach_count = ctx_count // 4
    query_pos = ctx_place * rows_per_shard + jnp.arange(rows_per_shard, dtype=jnp.int32)
    first_pos = trace_first(trace_lengths[0], query_pos)
    query_division = queries[0].reshape(rows_per_shard, KEY_VALUE_HEADS, head_groups, HEAD_SIZE)
    score_scale = 1.0 / math.sqrt(HEAD_SIZE)

    def attend(running, kv_piece, offset):
        key_portion, value_portion = kv_piece
        width = key_portion.shape[1]
        size_value = min(512, width)
        old_max, old_total, old_sum = running
        key_division = key_portion[0, 0:size_value].reshape(size_value, KEY_VALUE_HEADS, HEAD_SIZE)
        value_division = value_portion[0, 0:size_value].reshape(
            size_value, KEY_VALUE_HEADS, HEAD_SIZE
        )
        scores = (
            jnp.einsum(
                "tkgd,skd->kgts", query_division, key_division, preferred_element_type=jnp.float32
            )
            * score_scale
        )
        key_pos = offset + 0 + jnp.arange(size_value, dtype=jnp.int32)
        visible = (key_pos[None, :] <= query_pos[:, None]) & (
            key_pos[None, :] >= first_pos[:, None]
        )
        scores = jnp.where(visible, scores, -1e30)
        new_max = jnp.maximum(old_max, jnp.max(scores, axis=-1))
        weights = jnp.where(visible, jnp.exp(scores - new_max[..., None]), 0.0)
        rescale = jnp.exp(old_max - new_max)
        new_total = old_total * rescale + jnp.sum(weights, axis=-1)
        new_sum = old_sum * rescale[..., None] + jnp.einsum(
            "kgts,skd->kgtd",
            weights.astype(jnp.bfloat16),
            value_division,
            preferred_element_type=jnp.float32,
        )
        running = (new_max, new_total, new_sum)
        return running

    empty_state = (
        jnp.full((KEY_VALUE_HEADS, head_groups, rows_per_shard), -1e30, jnp.float32),
        jnp.zeros((KEY_VALUE_HEADS, head_groups, rows_per_shard), jnp.float32),
        jnp.zeros((KEY_VALUE_HEADS, head_groups, rows_per_shard, HEAD_SIZE), jnp.float32),
    )
    own_pair = jnp.stack([key_heads, value_head_array])
    own_state = attend(empty_state, (key_heads, value_head_array), ctx_place * rows_per_shard)

    def earlier_step(i, state):
        moving, running = state
        moving = shifted(moving, "ctx", 1)
        running = attend(running, (moving[0], moving[1]), (ctx_place - i - 1) * rows_per_shard)
        return (moving, running)

    final_state = lax.fori_loop(0, reach_count, earlier_step, (own_pair, own_state))[1]
    context = (
        (final_state[2] / final_state[1][..., None])
        .transpose(2, 0, 1, 3)
        .reshape(rows_per_shard, QUERY_HEADS * HEAD_SIZE)
    )
    mean_square = jnp.mean(context * context, axis=-1, keepdims=True)
    normed = (context * lax.rsqrt(mean_square + 1e-06) * norm_gain.astype(jnp.float32)).astype(
        jnp.bfloat16
    )
    chosen_ids = expert_ids[0]
    weight_rows = gate_weights[0]
    slot_range = jnp.arange(CAP, dtype=jnp.int32)
    placing_list = []
    mixing_list = []
    for e in range(EXP_WIN):
        chosen = chosen_ids == e
        routed = jnp.any(chosen, axis=-1)
        gate_value = jnp.sum(jnp.where(chosen, weight_rows, 0.0), axis=-1)
        slot_index = jnp.cumsum(routed.astype(jnp.int32)) - 1
        taken = (slot_index[None, :] == slot_range[:, None]) & routed[None, :]
        placing_list.append(taken.astype(jnp.bfloat16))
        mixing_list.append(jnp.where(taken.T, gate_value[:, None], 0.0))
    placing = jnp.concatenate(placing_list, axis=0)
    mixing = jnp.concatenate(mixing_list, axis=1)
    stacked = (
        jnp.dot(placing, normed, preferred_element_type=jnp.float32)
        .astype(jnp.bfloat16)
        .reshape(EXP_WIN, CAP, D)
    )
    expert_out = experts(stacked, w_gate, w_up, w_down)
    expert_mix = jnp.dot(
        mixing,
        expert_out.reshape(EXP_WIN * CAP, D),
        precision=lax.Precision.HIGHEST,
        preferred_element_type=jnp.float32,
    )
    return (context + expert_mix).astype(jnp.bfloat16)[None]


LANES = 128
PIECES = 2
SLOT_GROUPS = (6, 4)
MESH = pl.DeviceIdType.MESH


def fused(
    ctx_count,
    ep_count,
    ids_ref,
    gates_ref,
    lengths_ref,
    q_ref,
    k_ref,
    v_ref,
    gain_ref,
    row_meta_ref,
    slot_meta_ref,
    upper_ref,
    perm_a_ref,
    perm_b_ref,
    perm_t_a_ref,
    perm_t_b_ref,
    w_gate_hbm,
    w_up_hbm,
    w_down_hbm,
    out_ref,
    kv_prev,
    tops,
    totals,
    context,
    normed,
    tall,
    sent_rows,
    got_rows,
    flat,
    partial,
    got_partial,
    hidden,
    got_hidden,
    turned,
    sent_out,
    got_out,
    expert_out,
    mix,
    w_gate,
    w_up,
    w_down,
    w_sem,
    kv_send,
    kv_recv,
    rows_send,
    rows_recv,
    part_send,
    part_recv,
    hid_send,
    hid_recv,
    out_send,
    out_recv,
):
    f32, bf16 = jnp.float32, jnp.bfloat16
    c = lax.axis_index("ctx")
    e = lax.axis_index("ep")
    devices = ctx_count * ep_count
    tokens = q_ref.shape[0]
    wide = w_gate.shape[0]
    units = w_gate.shape[1]
    chunks = wide // LANES
    slots = ep_count * CAP
    piece = units // PIECES
    head_groups = QUERY_HEADS // KEY_VALUE_HEADS
    groups = range(len(SLOT_GROUPS))
    perms = (perm_a_ref, perm_b_ref)
    perms_t = (perm_t_a_ref, perm_t_b_ref)
    blocks = [chunks * size for size in SLOT_GROUPS]
    bases = [ep_count * chunks * sum(SLOT_GROUPS[:g]) for g in groups]
    slot_counts = [ep_count * size for size in SLOT_GROUPS]
    slot_bases = [ep_count * sum(SLOT_GROUPS[:g]) for g in groups]

    weight_copies = [
        pltpu.make_async_copy(hbm, vmem, w_sem.at[i])
        for i, (hbm, vmem) in enumerate(
            ((w_gate_hbm, w_gate), (w_up_hbm, w_up), (w_down_hbm, w_down))
        )
    ]
    for copy in weight_copies:
        copy.start()

    def peer(i):
        return lax.rem(c + i // ep_count, ctx_count), lax.rem(e + lax.rem(i, ep_count), ep_count)

    barrier = pltpu.get_barrier_semaphore()

    def greet(i, carry):
        pl.semaphore_signal(barrier, inc=1, device_id=peer(i), device_id_type=MESH)
        return carry

    lax.fori_loop(1, devices, greet, 0)
    square = (tokens, tokens)
    query_pos = c * tokens + lax.broadcasted_iota(jnp.int32, square, 0)
    key_pos = c * tokens + lax.broadcasted_iota(jnp.int32, square, 1)
    first_pos = jnp.zeros(square, jnp.int32)
    start = jnp.int32(0)
    for i in range(lengths_ref.shape[1]):
        first_pos = jnp.where(query_pos >= start, start, first_pos)
        start = start + lengths_ref[0, i]
    own_visible = (key_pos <= query_pos) & (key_pos >= first_pos)
    earlier_visible = key_pos - tokens >= first_pos
    score_scale = 1.0 / math.sqrt(HEAD_SIZE)

    def score(cols, keys, visible):
        scores = lax.dot_general(
            q_ref[:, cols], keys, (((1,), (1,)), ((), ())), preferred_element_type=f32
        )
        return jnp.where(visible, scores * score_scale, -1e30)

    def head_cols(head):
        return pl.ds(pl.multiple_of(head * HEAD_SIZE, HEAD_SIZE), HEAD_SIZE)

    for kv in range(KEY_VALUE_HEADS):
        kv_cols = slice(kv * HEAD_SIZE, (kv + 1) * HEAD_SIZE)

        def attend_own(h, carry, kv=kv, keys=k_ref[:, kv_cols], values=v_ref[:, kv_cols]):
            for one in range(4):
                head = kv * head_groups + h * 4 + one
                cols = head_cols(head)
                scores = score(cols, keys, own_visible)
                top = jnp.max(scores, axis=-1, keepdims=True)
                weights = jnp.where(own_visible, jnp.exp(scores - top), 0.0)
                total = jnp.sum(weights, axis=-1, keepdims=True)
                tops[head] = jnp.broadcast_to(top, (tokens, HEAD_SIZE))
                totals[head] = jnp.broadcast_to(total, (tokens, HEAD_SIZE))
                context[:, cols] = jnp.dot(
                    weights.astype(bf16), values, preferred_element_type=f32
                )
            return carry

        lax.fori_loop(0, head_groups // 4, attend_own, 0)

    pl.semaphore_wait(barrier, devices - 1)

    kv_copies = [
        pltpu.make_async_remote_copy(
            src_ref=ref,
            dst_ref=kv_prev.at[i],
            send_sem=kv_send.at[i],
            recv_sem=kv_recv.at[i],
            device_id=(lax.rem(c + 1, ctx_count), e),
            device_id_type=MESH,
        )
        for i, ref in enumerate((k_ref, v_ref))
    ]
    for copy in kv_copies:
        copy.start()

    hits = jnp.zeros((slots, tokens), f32)
    gate_at = jnp.zeros((slots, tokens), f32)
    for j in range(ids_ref.shape[0]):
        hit = ids_ref[j : j + 1, :] == slot_meta_ref[:, 0:1]
        hits += jnp.where(hit, 1.0, 0.0)
        gate_at += jnp.where(hit, gates_ref[j : j + 1, :], 0.0)
    count = jnp.dot(hits.astype(bf16), upper_ref[...], preferred_element_type=f32)
    gate_at = jnp.where(count.astype(jnp.int32) == slot_meta_ref[:, 1:2] + 1, gate_at, 0.0)
    high = gate_at.astype(bf16)
    mix[:, 0:tokens] = high
    mix[:, tokens : 2 * tokens] = (gate_at - high.astype(f32)).astype(bf16)

    named = jnp.zeros((chunks * slots, tokens), f32)
    for j in range(ids_ref.shape[0]):
        named += jnp.where(ids_ref[j : j + 1, :] == row_meta_ref[:, 0:1], 1.0, 0.0)
    count = jnp.dot(named.astype(bf16), upper_ref[...], preferred_element_type=f32)
    taken = jnp.where(count.astype(jnp.int32) == row_meta_ref[:, 2:3] + 1, named, 0.0)
    for k in range(chunks):
        tall[:, k * tokens : (k + 1) * tokens] = jnp.where(
            row_meta_ref[:, 1:2] == k, taken, 0.0
        ).astype(bf16)

    for copy in kv_copies:
        copy.wait()

    for kv in range(KEY_VALUE_HEADS):
        kv_cols = slice(kv * HEAD_SIZE, (kv + 1) * HEAD_SIZE)

        def attend_earlier(
            h, carry, kv=kv, keys=kv_prev[0, :, kv_cols], values=kv_prev[1, :, kv_cols]
        ):
            for one in range(4):
                head = kv * head_groups + h * 4 + one
                cols = head_cols(head)
                scores = score(cols, keys, earlier_visible)
                old_top = tops[head]
                top = jnp.maximum(old_top, jnp.max(scores, axis=-1, keepdims=True))
                weights = jnp.where(earlier_visible, jnp.exp(scores - top), 0.0)
                rescale = jnp.exp(old_top - top)
                total = totals[head] * rescale + jnp.sum(weights, axis=-1, keepdims=True)
                summed = jnp.dot(weights.astype(bf16), values, preferred_element_type=f32)
                context[:, cols] = (context[:, cols] * rescale + summed) / total
            return carry

        lax.fori_loop(0, head_groups // 4, attend_earlier, 0)

    def add_square(h, running):
        part = context[:, pl.ds(pl.multiple_of(h * HEAD_SIZE, HEAD_SIZE), HEAD_SIZE)]
        return running + part * part

    squares = lax.fori_loop(0, QUERY_HEADS, add_square, jnp.zeros((tokens, HEAD_SIZE), f32))
    inverse = lax.rsqrt(jnp.sum(squares, axis=-1, keepdims=True) * (1.0 / D) + 1e-06)
    for cc in range(ctx_count):
        for k in range(chunks):
            cols = slice(cc * wide + k * LANES, cc * wide + (k + 1) * LANES)
            normed[k * tokens : (k + 1) * tokens, cc * LANES : (cc + 1) * LANES] = (
                context[:, cols] * inverse * gain_ref[:, cols].astype(f32)
            ).astype(bf16)

    me = c * ep_count + e

    def rows_at(ref, g, cc, ee):
        return ref.at[cc, pl.ds(pl.multiple_of(bases[g] + ee * blocks[g], 16), blocks[g]), :]

    def exchange(g, i, source, target, send_sem, recv_sem):
        cc, ee = peer(i)
        return pltpu.make_async_remote_copy(
            src_ref=rows_at(source, g, cc, ee),
            dst_ref=rows_at(target, g, c, e),
            send_sem=send_sem.at[g, i],
            recv_sem=recv_sem.at[g, me],
            device_id=(cc, ee),
            device_id_type=MESH,
        )

    def arrival(g, i, source, target, send_sem, recv_sem):
        cc, ee = peer(i)
        return pltpu.make_async_remote_copy(
            src_ref=rows_at(source, g, cc, ee),
            dst_ref=rows_at(target, g, cc, ee),
            send_sem=send_sem.at[g, i],
            recv_sem=recv_sem.at[g, cc * ep_count + ee],
            device_id=(cc, ee),
            device_id_type=MESH,
        )

    def send_all(g, source, target, send_sem, recv_sem):
        def begin(i, carry):
            exchange(g, i, source, target, send_sem, recv_sem).start()
            return carry

        lax.fori_loop(1, devices, begin, 0)
        own = pl.ds(pl.multiple_of(bases[g] + e * blocks[g], 16), blocks[g])
        target[c, own, :] = source[c, own, :]

    def receive_all(g, source, target, send_sem, recv_sem):
        def end(i, carry):
            arrival(g, i, source, target, send_sem, recv_sem).wait_recv()
            return carry

        lax.fori_loop(1, devices, end, 0)

    def all_sent(g, source, target, send_sem, recv_sem):
        def end(i, carry):
            exchange(g, i, source, target, send_sem, recv_sem).wait_send()
            return carry

        lax.fori_loop(1, devices, end, 0)

    def unturned(g, ref):
        rows = slice(bases[g], bases[g] + ep_count * blocks[g])
        cat = jnp.concatenate([ref[cc, rows, :] for cc in range(ctx_count)], axis=1)
        return jnp.dot(perms[g][...], cat, preferred_element_type=f32).astype(bf16)

    row_set = (sent_rows, got_rows, rows_send, rows_recv)
    out_set = (sent_out, got_out, out_send, out_recv)
    others = [lax.rem(c + d, ctx_count) for d in range(1, ctx_count)]

    def part_copy(g, j, d, cc, slot):
        rows = pl.ds(slot_bases[g], slot_counts[g])
        return pltpu.make_async_remote_copy(
            src_ref=partial.at[j, cc, rows, :],
            dst_ref=got_partial.at[j, slot, rows, :],
            send_sem=part_send.at[g, j, d],
            recv_sem=part_recv.at[g, j, slot],
            device_id=(cc, e),
            device_id_type=MESH,
        )

    def hid_copy(g, j, d, cc, slot):
        rows = pl.ds(slot_bases[g], slot_counts[g])
        return pltpu.make_async_remote_copy(
            src_ref=hidden.at[j, rows, :],
            dst_ref=got_hidden.at[j, slot, rows, :],
            send_sem=hid_send.at[g, j, d],
            recv_sem=hid_recv.at[g, j, slot],
            device_id=(cc, e),
            device_id_type=MESH,
        )

    def place_rows(g):
        rows = slice(bases[g], bases[g] + ep_count * blocks[g])
        placed = jnp.dot(tall[rows, :], normed[...], preferred_element_type=f32).astype(bf16)
        for cc in range(ctx_count):
            sent_rows[cc, rows, :] = placed[:, cc * LANES : (cc + 1) * LANES]

    def multiply(g, send):
        receive_all(g, *row_set)
        if g == 0:
            send_all(1, *row_set)
        ordered = unturned(g, got_rows)
        count, base = slot_counts[g], slot_bases[g]
        first = ctx_count * base
        for cc in range(ctx_count):
            for k in range(chunks):
                flat[
                    first + cc * count : first + (cc + 1) * count, k * LANES : (k + 1) * LANES
                ] = ordered[k * count : (k + 1) * count, cc * LANES : (cc + 1) * LANES]
        if g == 0:
            weight_copies[0].wait()
            weight_copies[1].wait()
        rows = flat[first : first + ctx_count * count, :]
        for j in range(PIECES):
            cols = slice(j * piece, (j + 1) * piece)
            gate = jnp.dot(rows, w_gate[:, cols], preferred_element_type=f32).astype(bf16)
            up = jnp.dot(rows, w_up[:, cols], preferred_element_type=f32).astype(bf16)
            for cc in range(ctx_count):
                here = slice(cc * count, (cc + 1) * count)
                partial[j, cc, base : base + count, 0:piece] = gate[here]
                partial[j, cc, base : base + count, piece : 2 * piece] = up[here]
            if send:
                send_partial(g, j)

    def send_partial(g, j):
        for d, cc in enumerate(others):
            part_copy(g, j, d, cc, c).start()

    def activate(g):
        rows = pl.ds(slot_bases[g], slot_counts[g])
        for j in range(PIECES):
            proj = partial[j, c, rows, :].astype(f32)
            for d, cc in enumerate(others):
                part_copy(g, j, d, cc, cc).wait_recv()
                proj += got_partial[j, cc, rows, :].astype(f32)
            gate, up = proj[:, 0:piece], proj[:, piece : 2 * piece]
            units_here = (gate / (1.0 + jnp.exp(-gate)) * up).astype(bf16)
            hidden[j, rows, :] = units_here
            for d, cc in enumerate(others):
                hid_copy(g, j, d, cc, c).start()
            got_hidden[j, c, rows, :] = units_here

    def project_down(g):
        count, base = slot_counts[g], slot_bases[g]
        if g == 0:
            weight_copies[2].wait()
        down = jnp.zeros((ctx_count * count, wide), f32)
        for j in range(PIECES):
            for d, cc in enumerate(others):
                hid_copy(g, j, d, cc, cc).wait_recv()
            rows = jnp.concatenate(
                [got_hidden[j, cc, base : base + count, :] for cc in range(ctx_count)], axis=0
            )
            down += jnp.dot(
                rows, w_down[j * piece : (j + 1) * piece, :], preferred_element_type=f32
            )
        if g == 0:
            for j in range(PIECES):
                send_partial(1, j)
        down = down.astype(bf16)
        rows = slice(bases[g], bases[g] + ep_count * blocks[g])
        for cc in range(ctx_count):
            for k in range(chunks):
                turned[
                    bases[g] + k * count : bases[g] + (k + 1) * count,
                    cc * LANES : (cc + 1) * LANES,
                ] = down[cc * count : (cc + 1) * count, k * LANES : (k + 1) * LANES]
        back = jnp.dot(perms_t[g][...], turned[rows, :], preferred_element_type=f32).astype(bf16)
        for cc in range(ctx_count):
            sent_out[cc, rows, :] = back[:, cc * LANES : (cc + 1) * LANES]
        send_all(g, *out_set)

    def take_back(g):
        receive_all(g, *out_set)
        ordered = unturned(g, got_out)
        count, base = slot_counts[g], slot_bases[g]
        for cc in range(ctx_count):
            for k in range(chunks):
                cols = slice(cc * wide + k * LANES, cc * wide + (k + 1) * LANES)
                expert_out[base : base + count, cols] = ordered[
                    k * count : (k + 1) * count, cc * LANES : (cc + 1) * LANES
                ]

    place_rows(0)
    send_all(0, *row_set)
    place_rows(1)
    multiply(0, True)
    multiply(1, False)
    activate(0)
    project_down(0)
    activate(1)
    project_down(1)
    take_back(0)
    take_back(1)

    for cc in range(ctx_count):
        cols = slice(cc * wide, (cc + 1) * wide)
        mixed = lax.dot_general(
            mix[...], expert_out[:, cols], (((0,), (0,)), ((), ())), preferred_element_type=f32
        )
        out_ref[:, cols] = (context[:, cols] + mixed[0:tokens] + mixed[tokens:]).astype(bf16)

    for g in groups:
        all_sent(g, *row_set)
        all_sent(g, *out_set)
        for j in range(PIECES):
            for d, cc in enumerate(others):
                part_copy(g, j, d, cc, c).wait_send()
                hid_copy(g, j, d, cc, c).wait_send()


def local_fused(
    queries,
    key_heads,
    value_head_array,
    trace_lengths,
    expert_ids,
    gate_weights,
    norm_gain,
    w_gate,
    w_up,
    w_down,
):
    bf16 = jnp.bfloat16
    ctx_count, ep_count = lax.axis_size("ctx"), lax.axis_size("ep")
    tokens = queries.shape[1]
    wide, units = w_gate.shape
    chunks = wide // LANES
    slots = ep_count * CAP
    tall_rows = chunks * slots
    row_meta, slot_meta, perms = [], [], []
    for g, size in enumerate(SLOT_GROUPS):
        first = sum(SLOT_GROUPS[:g])
        n = np.arange(ep_count * chunks * size)
        row_e, row_k, row_s = n // (chunks * size), n // size % chunks, n % size
        row_meta.append(np.stack([row_e, row_k, row_s + first], axis=1).astype(np.int32))
        m = np.arange(ep_count * size)
        slot_meta.append(np.stack([m // size, m % size + first], axis=1).astype(np.int32))
        perm = np.zeros((n.size, n.size), np.float32)
        perm[(row_k * ep_count + row_e) * size + row_s, n] = 1.0
        perms.append(perm)
    row_meta, slot_meta = np.concatenate(row_meta), np.concatenate(slot_meta)
    upper = np.triu(np.ones((tokens, tokens), np.float32))
    vmem = pl.BlockSpec(memory_space=pltpu.VMEM)
    anywhere = pl.BlockSpec(memory_space=pl.ANY)
    dma = pltpu.SemaphoreType.DMA
    devices = ctx_count * ep_count
    groups = len(SLOT_GROUPS)
    piece = units // PIECES
    across = ctx_count * LANES
    out = pl.pallas_call(
        functools.partial(fused, ctx_count, ep_count),
        out_shape=jax.ShapeDtypeStruct((tokens, D), bf16),
        in_specs=[vmem] * 2
        + [pl.BlockSpec(memory_space=pltpu.SMEM)]
        + [vmem] * 11
        + [anywhere] * 3,
        out_specs=vmem,
        scratch_shapes=[
            pltpu.VMEM((2, tokens, KEY_VALUE_HEADS * HEAD_SIZE), bf16),
            pltpu.VMEM((QUERY_HEADS, tokens, HEAD_SIZE), jnp.float32),
            pltpu.VMEM((QUERY_HEADS, tokens, HEAD_SIZE), jnp.float32),
            pltpu.VMEM((tokens, D), jnp.float32),
            pltpu.VMEM((chunks * tokens, across), bf16),
            pltpu.VMEM((tall_rows, chunks * tokens), bf16),
            pltpu.VMEM((ctx_count, tall_rows, LANES), bf16),
            pltpu.VMEM((ctx_count, tall_rows, LANES), bf16),
            pltpu.VMEM((ctx_count * slots, wide), bf16),
            pltpu.VMEM((PIECES, ctx_count, slots, 2 * piece), bf16),
            pltpu.VMEM((PIECES, ctx_count, slots, 2 * piece), bf16),
            pltpu.VMEM((PIECES, slots, piece), bf16),
            pltpu.VMEM((PIECES, ctx_count, slots, piece), bf16),
            pltpu.VMEM((tall_rows, across), bf16),
            pltpu.VMEM((ctx_count, tall_rows, LANES), bf16),
            pltpu.VMEM((ctx_count, tall_rows, LANES), bf16),
            pltpu.VMEM((slots, D), bf16),
            pltpu.VMEM((slots, 2 * tokens), bf16),
            pltpu.VMEM((wide, units), bf16),
            pltpu.VMEM((wide, units), bf16),
            pltpu.VMEM((units, wide), bf16),
            dma((3,)),
            dma((2,)),
            dma((2,)),
            dma((groups, devices)),
            dma((groups, devices)),
            dma((groups, PIECES, ctx_count)),
            dma((groups, PIECES, ctx_count)),
            dma((groups, PIECES, ctx_count)),
            dma((groups, PIECES, ctx_count)),
            dma((groups, devices)),
            dma((groups, devices)),
        ],
        compiler_params=pltpu.CompilerParams(
            collective_id=0, has_side_effects=True, vmem_limit_bytes=56 * 1024 * 1024
        ),
        cost_estimate=pl.CostEstimate(
            flops=4_000_000_000, bytes_accessed=14_000_000, transcendentals=1_000_000
        ),
    )(
        expert_ids[0].T,
        gate_weights[0].T,
        trace_lengths,
        queries[0],
        key_heads[0],
        value_head_array[0],
        norm_gain[None],
        row_meta,
        slot_meta,
        upper.astype(bf16),
        perms[0].astype(bf16),
        perms[1].astype(bf16),
        perms[0].T.astype(bf16),
        perms[1].T.astype(bf16),
        w_gate,
        w_up,
        w_down,
    )
    return out[None]


def local(*args):
    ctx_count, ep_count = lax.axis_size("ctx"), lax.axis_size("ep")
    wide, units = args[7].shape
    aligned = all((wide // LANES * size) % 16 == 0 for size in SLOT_GROUPS) and units % (PIECES * LANES) == 0
    aligned = aligned and args[0].shape[1] == HEAD_SIZE
    if ep_count == EXP_WIN and ctx_count == 4 and aligned:
        return local_fused(*args)
    return local_plain(*args)


def solution(mesh):
    in_specs = (
        P("ep", "ctx", None),
        P("ep", "ctx", None),
        P("ep", "ctx", None),
        P("ep", None),
        P("ep", "ctx", None),
        P("ep", "ctx", None),
        P(),
        P("ctx", "ep"),
        P("ctx", "ep"),
        P("ep", "ctx"),
    )
    out_specs = P("ep", "ctx", None)
    return jax.shard_map(local, mesh=mesh, in_specs=in_specs, out_specs=out_specs, check_vma=False)
```
